128 devices in a mesh: hi: 4 (over z_hi, core), lo: 32 (over y, z_lo, x).
Axes of the slice: x: 4, y: 4, z: 4 (z_hi: 2, z_lo: 2; z = z_hi * 2 + z_lo), core: 2. Of those that a mesh axis runs over, the one named last changes fastest.
Arguments:
- sources: bfloat16 [2, 256, 1048576], P(None, None, ('hi', 'lo')), may hold values from -6 to 6
- source_map: bfloat16 [64, 256], replicated, may hold values from -0.375 to 0.375
- translation: bfloat16 [15, 2, 64, 128], replicated, may hold values from -0.5 to 0.5
- box_gain: float32 [15, 1048576], P(None, ('hi', 'lo')), may hold values from 0.5 to 1.5
- target_order: int32 [128, 8192], P(('hi', 'lo')), may hold values from 0 to 8191, each once within a row
- target_map: bfloat16 [256, 64], replicated, may hold values from -0.75 to 0.75
Outputs:
- field: bfloat16 [2, 256, 1048576], P(None, None, ('hi', 'lo'))
The draws below stay inside these ranges and needn't reach their ends.
Inputs may be any that keep to these rules, and one draw needn't show every extreme that they name: Each row of target_order holds every number of 0 to 8191 once.
All inputs are finite; a program needn't handle non-finite values.
Results may differ from the reference program's by a relative error of at most 0.03.
Values may be sent and summed in bfloat16 or wider, within the bound.
No kernel may reach another device: no remote copies, remote signals or barrier semaphores. Data moves between devices by JAX's collectives and lax.ppermute only.
A program may use at most 128 MiB of HBM per device.

```python
import jax
import jax.numpy as jnp

RANK = 64
LEAF_PTS = 256
IMAGES = 2
LOCAL_LEVELS = 8
BOX_DEV = 8192
LEVELS_HI = 2
LEVELS_LO = 5
LEVELS = 15
BOXES = 1048576
N_HI = 4
N_LO = 32


def block_scale(own_key, shape, split, smallest, high):
    def one(position, shards_of):
        draws = jax.random.uniform(jax.random.fold_in(jax.random.fold_in(own_key, 6), position), (shards_of,), jnp.float32, smallest / len(split), high / len(split))
        return jnp.repeat(jnp.exp(draws), shape[position] // shards_of).reshape((-1,) + (1,) * (len(shape) - position - 1))

    gain = one(*split[0])
    for cut in split[1:]:
        gain = gain * one(*cut)
    return gain


def scatter_about(key, shape, deviation, reach, split=(), held_as=jnp.bfloat16):
    gain = block_scale(key, shape, split, -0.22, 0.18) if split else 1.0
    entries = jax.random.normal(key, shape, jnp.float32) * deviation * gain
    return jnp.minimum(jnp.maximum(entries, -reach), reach).astype(held_as)


def setup_inputs(seed: int = 0) -> dict:
    key_list = jax.random.split(jax.random.key(seed), 7)
    sources = scatter_about(key_list[0], (IMAGES, LEAF_PTS, BOXES), 1.0, 6.0, ((2, 128),))
    source_map = scatter_about(key_list[1], (RANK, LEAF_PTS), LEAF_PTS ** -0.5, 0.375)
    translation = scatter_about(key_list[2], (LEVELS, 2, RANK, 2 * RANK), (2 * RANK) ** -0.5, 0.5)
    box_gain = jnp.clip(1.0 + 0.1 * jax.random.normal(key_list[3], (LEVELS, BOXES), jnp.float32), 0.5, 1.5)
    target_order = jax.vmap(lambda own: jax.random.permutation(own, BOX_DEV))(jax.random.split(key_list[4], (N_HI * N_LO))).reshape((N_HI * N_LO, BOX_DEV)).astype(jnp.int32)
    target_map = scatter_about(key_list[5], (LEAF_PTS, RANK), RANK ** -0.5, 0.75)
    return dict(sources=sources, source_map=source_map, translation=translation, box_gain=box_gain, target_order=target_order, target_map=target_map)


def arrange(product, ranks):
    shaped = product.reshape((product.shape[0], 2, ranks) + product.shape[2:])
    moved = jnp.moveaxis(shaped, 1, -2)
    return moved.reshape(moved.shape[:-2] + (2 * moved.shape[-1],))


def combine(matrix, low_part, high_part):
    square = matrix.reshape(2 * RANK, 2 * RANK).astype(jnp.float32)
    stacked = jnp.concatenate([low_part, high_part], axis=1).astype(jnp.float32)
    product = jnp.einsum('ok,ck...->co...', square, stacked)
    return arrange(product, RANK)


def scaled(result, box_gain, level_no, lead):
    return (result * box_gain[level_no].reshape(lead, BOX_DEV)).astype(jnp.bfloat16)


def cross(weights, matrix, bit_pos):
    lead = weights.shape[2]
    inner = 2 ** bit_pos
    outer = lead // (2 * inner)
    shaped = weights.reshape(IMAGES, RANK, outer, 2, inner, BOX_DEV)
    low_part = shaped[:, :, :, 0]
    high_part = shaped[:, :, :, 1]
    half_size = BOX_DEV // 2
    sides = []
    for side_no in range(2):
        lower = low_part[..., side_no * half_size:(side_no + 1) * half_size]
        upper = high_part[..., side_no * half_size:(side_no + 1) * half_size]
        sides.append(combine(matrix, lower, upper))
    return jnp.stack(sides, axis=3).reshape(IMAGES, RANK, lead, BOX_DEV)


def reference(sources, source_map, translation, box_gain, target_order, target_map):
    lead = N_HI * N_LO
    weights = jnp.einsum('rs,csg->crg', source_map.astype(jnp.float32), sources.astype(jnp.float32))
    weights = weights.astype(jnp.bfloat16).reshape(IMAGES, RANK, lead, BOX_DEV)
    half_size = BOX_DEV // 2
    level_no = 0
    for step_no in range(LOCAL_LEVELS):
        result = combine(translation[level_no], weights[..., :half_size], weights[..., half_size:])
        weights = scaled(result, box_gain, level_no, lead)
        level_no += 1
    for step_no in range(LEVELS_HI):
        result = cross(weights, translation[level_no], LEVELS_LO + LEVELS_HI - 1 - step_no)
        weights = scaled(result, box_gain, level_no, lead)
        level_no += 1
    piece = BOX_DEV // N_LO
    moved = weights.reshape(IMAGES, RANK, N_HI, N_LO, N_LO, piece)
    moved = jnp.swapaxes(moved, 3, 4).reshape(IMAGES, RANK, lead, BOX_DEV)
    order = target_order.astype(jnp.int32)[None, None]
    weights = jnp.take_along_axis(moved, order, axis=3)
    for step_no in range(LEVELS_LO):
        result = cross(weights, translation[level_no], LEVELS_LO - 1 - step_no)
        weights = scaled(result, box_gain, level_no, lead)
        level_no += 1
    weights = weights.reshape(IMAGES, RANK, lead * BOX_DEV)
    field = jnp.einsum('sr,crg->csg', target_map.astype(jnp.float32), weights.astype(jnp.float32))
    return field.astype(jnp.bfloat16)
```

```python
import functools

import jax
import jax.numpy as jnp
from jax import lax
from jax.experimental import pallas as pl
from jax.experimental.pallas import tpu as pltpu
from jax.sharding import PartitionSpec as P

LOCAL_LEVELS = 8
F32 = jnp.float32
BF16 = jnp.bfloat16
VMEM_LIMIT = 48 * 2**20


def dot(a, b):
    return jnp.dot(a, b, preferred_element_type=F32)


def pick(own, kept, received):
    first = own == 0
    return jnp.where(first, kept, received), jnp.where(first, received, kept)


def pair(matrix, low, high, gains):
    ranks = low.shape[0]
    product = dot(matrix, jnp.concatenate([low, high], axis=0))
    return (
        (product[:ranks] * gains[0]).astype(BF16),
        (product[ranks:] * gains[1]).astype(BF16),
    )


def front_kernel(levels, own_ref, low_ref, high_ref, map_ref, tr_ref, gl_ref, gh_ref, kept_ref, sent_ref):
    own = own_ref[0]
    images = low_ref.shape[0]
    source_map = map_ref[...]
    for c in range(images):
        low = dot(source_map, low_ref[c]).astype(BF16)
        high = dot(source_map, high_ref[c]).astype(BF16)
        for level in range(levels):
            gains = gl_ref[level : level + 1, :], gh_ref[level : level + 1, :]
            low, high = pair(tr_ref[level], low, high, gains)
        kept_ref[c], sent_ref[c] = pick(own, low, high)


def front(own, sources, source_map, matrices, box_gain, cols):
    images, points, boxes = sources.shape
    ranks = source_map.shape[0]
    half = boxes // 2
    steps = half // cols
    levels = matrices.shape[0]
    grid_spec = pltpu.PrefetchScalarGridSpec(
        num_scalar_prefetch=1,
        grid=(steps,),
        in_specs=[
            pl.BlockSpec((images, points, cols), lambda i, s: (0, 0, i)),
            pl.BlockSpec((images, points, cols), lambda i, s: (0, 0, i + steps)),
            pl.BlockSpec((ranks, points), lambda i, s: (0, 0)),
            pl.BlockSpec(matrices.shape, lambda i, s: (0, 0, 0)),
            pl.BlockSpec((box_gain.shape[0], cols), lambda i, s: (0, i)),
            pl.BlockSpec((box_gain.shape[0], cols), lambda i, s: (0, i + steps)),
        ],
        out_specs=[pl.BlockSpec((images, ranks, cols), lambda i, s: (0, 0, i))] * 2,
    )
    return pl.pallas_call(
        functools.partial(front_kernel, LOCAL_LEVELS),
        grid_spec=grid_spec,
        out_shape=[jax.ShapeDtypeStruct((images, ranks, half), BF16)] * 2,
        compiler_params=pltpu.CompilerParams(vmem_limit_bytes=VMEM_LIMIT),
        name="source_map_and_local_levels",
    )(own, sources, sources, source_map, matrices, box_gain, box_gain)


def swap_kernel(level, own_ref, kept_in, recv_in, tr_ref, gl_ref, gh_ref, kept_ref, sent_ref):
    images = kept_in.shape[0]
    gains = gl_ref[level : level + 1, :], gh_ref[level : level + 1, :]
    for c in range(images):
        low, high = pick(own_ref[0], kept_in[c], recv_in[c])
        low, high = pair(tr_ref[level], low, high, gains)
        kept_ref[c], sent_ref[c] = pick(own_ref[1], low, high)


def swap_level(level, owns, kept, received, matrices, box_gain, cols):
    images, ranks, half = kept.shape
    steps = half // cols
    block = pl.BlockSpec((images, ranks, cols), lambda i, s: (0, 0, i))
    grid_spec = pltpu.PrefetchScalarGridSpec(
        num_scalar_prefetch=1,
        grid=(steps,),
        in_specs=[
            block,
            block,
            pl.BlockSpec(matrices.shape, lambda i, s: (0, 0, 0)),
            pl.BlockSpec((box_gain.shape[0], cols), lambda i, s: (0, i)),
            pl.BlockSpec((box_gain.shape[0], cols), lambda i, s: (0, i + steps)),
        ],
        out_specs=[block] * 2,
    )
    return pl.pallas_call(
        functools.partial(swap_kernel, level),
        grid_spec=grid_spec,
        out_shape=[jax.ShapeDtypeStruct(kept.shape, BF16)] * 2,
        compiler_params=pltpu.CompilerParams(vmem_limit_bytes=VMEM_LIMIT),
        name="upper_level",
    )(owns, kept, received, matrices, box_gain, box_gain)


def rows_kernel(level, own_ref, kept_in, recv_in, tr_ref, gl_ref, gh_ref, out_ref):
    images = kept_in.shape[0]
    gains = gl_ref[level : level + 1, :], gh_ref[level : level + 1, :]
    lows, highs = [], []
    for c in range(images):
        low, high = pick(own_ref[0], kept_in[c], recv_in[c])
        low, high = pair(tr_ref[level], low, high, gains)
        lows.append(low)
        highs.append(high)
    piece = out_ref.shape[2]
    for n, parts in enumerate((lows, highs)):
        stacked = jnp.concatenate(parts, axis=0).astype(F32)
        for k in range(out_ref.shape[1]):
            out_ref[n, k] = stacked[:, k * piece : (k + 1) * piece].T.astype(BF16)


def rows_level(level, owns, kept, received, matrices, box_gain, cols, pieces):
    images, ranks, half = kept.shape
    steps = half // cols
    piece = 2 * half // pieces
    block = pl.BlockSpec((images, ranks, cols), lambda i, s: (0, 0, i))
    grid_spec = pltpu.PrefetchScalarGridSpec(
        num_scalar_prefetch=1,
        grid=(steps,),
        in_specs=[
            block,
            block,
            pl.BlockSpec(matrices.shape, lambda i, s: (0, 0, 0)),
            pl.BlockSpec((box_gain.shape[0], cols), lambda i, s: (0, i)),
            pl.BlockSpec((box_gain.shape[0], cols), lambda i, s: (0, i + steps)),
        ],
        out_specs=pl.BlockSpec((2, cols // piece, piece, images * ranks), lambda i, s: (0, i, 0, 0)),
    )
    out = pl.pallas_call(
        functools.partial(rows_kernel, level),
        grid_spec=grid_spec,
        out_shape=jax.ShapeDtypeStruct((2, pieces // 2, piece, images * ranks), BF16),
        compiler_params=pltpu.CompilerParams(vmem_limit_bytes=VMEM_LIMIT),
        name="upper_level_to_rows",
    )(owns, kept, received, matrices, box_gain, box_gain)
    return out.reshape(pieces, piece, images * ranks)


UNROLL = 32


def gather_kernel(order_ref, rows_ref, out_ref, table, picked):
    boxes = table.shape[0]
    chunk = 256

    def widen(i, carry):
        at = pl.ds(pl.multiple_of(i * chunk, chunk), chunk)
        table[at, :] = rows_ref[at, :].astype(F32)
        return carry

    lax.fori_loop(0, boxes // chunk, widen, 0)

    def move(i, carry):
        base = pl.multiple_of(i * UNROLL, UNROLL)
        for k in range(UNROLL):
            picked[pl.ds(base + k, 1), :] = table[pl.ds(order_ref[0, base + k], 1), :]
        return carry

    lax.fori_loop(0, boxes // UNROLL, move, 0)

    def narrow(i, carry):
        at = pl.ds(pl.multiple_of(i * chunk, chunk), chunk)
        out_ref[at, :] = picked[at, :].astype(BF16)
        return carry

    lax.fori_loop(0, boxes // chunk, narrow, 0)


def gather_rows(order, rows):
    boxes, width = rows.shape
    return pl.pallas_call(
        gather_kernel,
        in_specs=[
            pl.BlockSpec(memory_space=pltpu.SMEM),
            pl.BlockSpec(memory_space=pltpu.VMEM),
        ],
        out_specs=pl.BlockSpec(memory_space=pltpu.VMEM),
        out_shape=jax.ShapeDtypeStruct((boxes, width), BF16),
        scratch_shapes=[pltpu.VMEM((boxes, width), F32), pltpu.VMEM((boxes, width), F32)],
        compiler_params=pltpu.CompilerParams(vmem_limit_bytes=VMEM_LIMIT),
        name="box_order",
    )(order, rows)


def lower_kernel(levels, first, x_ref, tr_ref, gain_ref, out_ref, held):
    devices, cols, _ = x_ref.shape
    images, ranks = out_ref.shape[1], out_ref.shape[2]
    for i in range(levels):
        bit = levels - 1 - i
        matrix = tr_ref[first + i]
        if i == 0:
            blank = jnp.zeros((2 * ranks, ranks), BF16)
            sides = []
            for side in range(2):
                part = matrix[:, side * ranks : (side + 1) * ranks]
                bands = [
                    jnp.concatenate([part if c == b else blank for b in range(images)], axis=1)
                    for c in range(images)
                ]
                sides.append(jnp.concatenate(bands, axis=0))
            both = jnp.concatenate(sides, axis=1)
        target = out_ref if i == levels - 1 else held

        def group(g, carry):
            low_at = ((g >> bit) << (bit + 1)) | (g & ((1 << bit) - 1))
            high_at = low_at + (1 << bit)
            gains = gain_ref[g, 2 * i : 2 * i + 1, :], gain_ref[g, 2 * i + 1 : 2 * i + 2, :]
            if i == 0:
                stacked = jnp.concatenate([x_ref[low_at], x_ref[high_at]], axis=1)
                product = lax.dot_general(
                    both, stacked, (((1,), (1,)), ((), ())), preferred_element_type=F32
                )
            for c in range(images):
                if i == 0:
                    own = product[c * 2 * ranks : (c + 1) * 2 * ranks]
                else:
                    own = dot(matrix, jnp.concatenate([held[low_at, c], held[high_at, c]], axis=0))
                target[low_at, c] = (own[:ranks] * gains[0].astype(F32)).astype(BF16)
                target[high_at, c] = (own[ranks:] * gains[1].astype(F32)).astype(BF16)
            return carry

        lax.fori_loop(0, devices // 2, group, 0, unroll=2)


def lower_levels(x, matrices, gains, images, first):
    devices, cols, width = x.shape
    ranks = width // images
    levels = devices.bit_length() - 1
    shape = (devices, images, ranks, cols)
    return pl.pallas_call(
        functools.partial(lower_kernel, levels, first),
        in_specs=[pl.BlockSpec(memory_space=pltpu.VMEM)] * 3,
        out_specs=pl.BlockSpec(memory_space=pltpu.VMEM),
        out_shape=jax.ShapeDtypeStruct(shape, BF16),
        scratch_shapes=[pltpu.VMEM(shape, BF16)],
        compiler_params=pltpu.CompilerParams(vmem_limit_bytes=VMEM_LIMIT),
        name="lower_levels",
    )(x, matrices, gains)


def target_kernel(x_ref, map_ref, out_ref):
    pieces, _, images, ranks, cols = x_ref.shape
    target_map = map_ref[...]
    for k in range(pieces):
        for c in range(images):
            out_ref[c, :, k * cols : (k + 1) * cols] = dot(target_map, x_ref[k, 0, c]).astype(BF16)


def to_targets(x, target_map, pieces):
    t_pieces, two, images, ranks, cols = x.shape
    points = target_map.shape[0]
    per_half = t_pieces // pieces
    return pl.pallas_call(
        target_kernel,
        grid=(two, per_half),
        in_specs=[
            pl.BlockSpec((pieces, 1, images, ranks, cols), lambda n, i: (i, n, 0, 0, 0)),
            pl.BlockSpec((points, ranks), lambda n, i: (0, 0)),
        ],
        out_specs=pl.BlockSpec((images, points, pieces * cols), lambda n, i: (0, 0, n * per_half + i)),
        out_shape=jax.ShapeDtypeStruct((images, points, two * t_pieces * cols), BF16),
        compiler_params=pltpu.CompilerParams(vmem_limit_bytes=VMEM_LIMIT),
        name="target_map",
    )(x, target_map)


def body(sources, source_map, translation, box_gain, target_order, target_map):
    images, _, boxes = sources.shape
    ranks = source_map.shape[0]
    n_lower = lax.axis_size("lo")
    matrices = translation.reshape(translation.shape[0], 2 * ranks, 2 * ranks)
    upper = lax.axis_index("hi")
    owns = jnp.stack([upper >> 1 & 1, upper & 1]).astype(jnp.int32)
    first_lower = LOCAL_LEVELS + 2
    levels_lo = n_lower.bit_length() - 1
    piece = boxes // n_lower
    halves = n_lower // 2

    gains = box_gain[first_lower:].astype(BF16).reshape(levels_lo, 2, halves, piece)
    gains = gains.transpose(2, 0, 1, 3).reshape(halves, 2 * levels_lo, piece)
    groups = [list(range(halves)), list(range(halves, n_lower))]
    gains = lax.all_to_all(gains, "lo", 0, 0, axis_index_groups=groups)

    kept, sent = front(owns[:1], sources, source_map, matrices, box_gain, 512)
    received = lax.ppermute(sent, "hi", [(i, i ^ 2) for i in range(4)])
    kept, sent = swap_level(LOCAL_LEVELS, owns, kept, received, matrices, box_gain, 2048)
    received = lax.ppermute(sent, "hi", [(i, i ^ 1) for i in range(4)])
    rows = rows_level(LOCAL_LEVELS + 1, owns[1:], kept, received, matrices, box_gain, 1024, n_lower)
    rows = lax.all_to_all(rows, "lo", 0, 0)
    rows = gather_rows(target_order, rows.reshape(boxes, images * ranks))
    rows = lax.all_to_all(rows.reshape(n_lower, piece, images * ranks), "lo", 0, 0)
    blocks = lower_levels(rows, matrices, gains, images, first_lower)
    blocks = blocks.reshape(halves, 2, images, ranks, piece)
    blocks = lax.all_to_all(blocks, "lo", 0, 0, axis_index_groups=groups)
    return to_targets(blocks, target_map, 4)


def solution(mesh):
    return jax.shard_map(
        body,
        mesh=mesh,
        in_specs=(
            P(None, None, ("hi", "lo")),
            P(),
            P(),
            P(None, ("hi", "lo")),
            P(("hi", "lo"), None),
            P(),
        ),
        out_specs=P(None, None, ("hi", "lo")),
        check_vma=False,
    )
```

```python
import functools

import jax
import jax.numpy as jnp
from jax import lax
from jax.experimental import pallas as pl
from jax.experimental.pallas import tpu as pltpu
from jax.sharding import PartitionSpec as P

LOCAL_LEVELS = 8
F32 = jnp.float32
BF16 = jnp.bfloat16
VMEM_LIMIT = 40 * 2**20


def dot(a, b):
    return jnp.dot(a, b, preferred_element_type=F32)


def params(limit=VMEM_LIMIT):
    return pltpu.CompilerParams(vmem_limit_bytes=limit)


def cost(macs, moved):
    return pl.CostEstimate(flops=2 * macs, bytes_accessed=moved, transcendentals=0)


def pick(own, kept, received):
    first = own == 0
    return jnp.where(first, kept, received), jnp.where(first, received, kept)


def pair(matrix, low, high, gains):
    ranks = low.shape[0]
    product = dot(matrix, jnp.concatenate([low, high], axis=0))
    return (
        (product[:ranks] * gains[0]).astype(BF16),
        (product[ranks:] * gains[1]).astype(BF16),
    )


def front_kernel(levels, own_ref, low_ref, high_ref, map_ref, tr_ref, gl_ref, gh_ref, kept_ref, sent_ref):
    source_map = map_ref[...]
    low = dot(source_map, low_ref[0]).astype(BF16)
    high = dot(source_map, high_ref[0]).astype(BF16)
    for level in range(levels):
        gains = gl_ref[level : level + 1, :], gh_ref[level : level + 1, :]
        low, high = pair(tr_ref[level], low, high, gains)
    kept_ref[...], sent_ref[...] = pick(own_ref[0], low, high)


def front(image, own, sources, source_map, matrices, box_gain, cols):
    _, points, boxes = sources.shape
    ranks = source_map.shape[0]
    half = boxes // 2
    steps = half // cols
    grid_spec = pltpu.PrefetchScalarGridSpec(
        num_scalar_prefetch=1,
        grid=(steps,),
        in_specs=[
            pl.BlockSpec((1, points, cols), lambda i, s: (image, 0, i)),
            pl.BlockSpec((1, points, cols), lambda i, s: (image, 0, i + steps)),
            pl.BlockSpec((ranks, points), lambda i, s: (0, 0)),
            pl.BlockSpec(matrices.shape, lambda i, s: (0, 0, 0)),
            pl.BlockSpec((box_gain.shape[0], cols), lambda i, s: (0, i)),
            pl.BlockSpec((box_gain.shape[0], cols), lambda i, s: (0, i + steps)),
        ],
        out_specs=[pl.BlockSpec((ranks, cols), lambda i, s: (0, i))] * 2,
    )
    return pl.pallas_call(
        functools.partial(front_kernel, LOCAL_LEVELS),
        grid_spec=grid_spec,
        out_shape=[jax.ShapeDtypeStruct((ranks, half), BF16)] * 2,
        compiler_params=params(56 * 2**20),
        cost_estimate=cost(boxes * ranks * (points + LOCAL_LEVELS * 2 * ranks) * 8, boxes * points * 2),
        name="source_map_and_local_levels",
    )(own, sources, sources, source_map, matrices, box_gain, box_gain)


def swap_kernel(level, own_ref, kept_in, recv_in, tr_ref, gl_ref, gh_ref, kept_ref, sent_ref):
    gains = gl_ref[level : level + 1, :], gh_ref[level : level + 1, :]
    low, high = pick(own_ref[0], kept_in[...], recv_in[...])
    low, high = pair(tr_ref[level], low, high, gains)
    kept_ref[...], sent_ref[...] = pick(own_ref[1], low, high)


def pieces_kernel(level, own_ref, kept_in, recv_in, tr_ref, gl_ref, gh_ref, out_ref):
    gains = gl_ref[level : level + 1, :], gh_ref[level : level + 1, :]
    low, high = pick(own_ref[0], kept_in[...], recv_in[...])
    both = pair(tr_ref[level], low, high, gains)
    ranks = low.shape[0]
    piece = out_ref.shape[3]
    extra = out_ref.shape[2] - ranks
    if extra:
        later = [ref[i : i + 1, :] for i in range(level + 1, gl_ref.shape[0]) for ref in (gl_ref, gh_ref)]
        later += [jnp.zeros_like(later[0])] * (extra - len(later))
        later = jnp.concatenate(later, axis=0).astype(BF16)
    for n in range(2):
        for k in range(out_ref.shape[1]):
            at = slice(k * piece, (k + 1) * piece)
            out_ref[n, k, :ranks, :] = both[n][:, at]
            if extra:
                out_ref[n, k, ranks:, :] = later[:, at]


def upper_level(level, owns, kept, received, matrices, box_gain, cols, pieces=None, extra=0):
    ranks, half = kept.shape
    steps = half // cols
    block = pl.BlockSpec((ranks, cols), lambda i, s: (0, i))
    if pieces is None:
        kernel, out_specs = swap_kernel, [block] * 2
        out_shape = [jax.ShapeDtypeStruct(kept.shape, BF16)] * 2
    else:
        piece = 2 * half // pieces
        kernel = pieces_kernel
        out_specs = pl.BlockSpec((2, cols // piece, ranks + extra, piece), lambda i, s: (0, i, 0, 0))
        out_shape = jax.ShapeDtypeStruct((2, pieces // 2, ranks + extra, piece), BF16)
    grid_spec = pltpu.PrefetchScalarGridSpec(
        num_scalar_prefetch=1,
        grid=(steps,),
        in_specs=[
            block,
            block,
            pl.BlockSpec(matrices.shape, lambda i, s: (0, 0, 0)),
            pl.BlockSpec((box_gain.shape[0], cols), lambda i, s: (0, i)),
            pl.BlockSpec((box_gain.shape[0], cols), lambda i, s: (0, i + steps)),
        ],
        out_specs=out_specs,
    )
    return pl.pallas_call(
        functools.partial(kernel, level),
        grid_spec=grid_spec,
        out_shape=out_shape,
        compiler_params=params(),
        cost_estimate=cost(half * 4 * ranks * ranks * 8, half * ranks * 8),
        name="upper_level",
    )(owns, kept, received, matrices, box_gain, box_gain)


UNROLL = 32


def gather_kernel(order_ref, in_ref, out_ref, table, picked):
    pieces, _, piece = in_ref.shape

    def widen(i, carry):
        at = pl.ds(pl.multiple_of(i * piece, piece), piece)
        table[at, :] = in_ref[i, : table.shape[1], :].astype(F32).T
        return carry

    lax.fori_loop(0, pieces, widen, 0, unroll=2)

    def move(i, carry):
        base = pl.multiple_of(i * UNROLL, UNROLL)
        for k in range(UNROLL):
            picked[pl.ds(base + k, 1), :] = table[pl.ds(order_ref[0, base + k], 1), :]
        return carry

    lax.fori_loop(0, pieces * piece // UNROLL, move, 0)

    def narrow(i, carry):
        at = pl.ds(pl.multiple_of(i * piece, piece), piece)
        out_ref[i] = picked[at, :].T.astype(BF16)
        return carry

    lax.fori_loop(0, pieces, narrow, 0, unroll=2)


def gather(order, x, ranks):
    pieces, _, piece = x.shape
    return pl.pallas_call(
        gather_kernel,
        in_specs=[
            pl.BlockSpec(memory_space=pltpu.SMEM),
            pl.BlockSpec(memory_space=pltpu.VMEM),
        ],
        out_specs=pl.BlockSpec(memory_space=pltpu.VMEM),
        out_shape=jax.ShapeDtypeStruct((pieces, ranks, piece), BF16),
        scratch_shapes=[pltpu.VMEM((pieces * piece, ranks), F32)] * 2,
        compiler_params=params(),
        cost_estimate=cost(0, 30 * 2**20),
        name="box_order",
    )(order, x)


def lower_kernel(levels, first, own_ref, x_ref, tr_ref, gain_ref, out_ref, held):
    devices, ranks, _ = x_ref.shape
    half_at = own_ref[0] * (devices // 2)
    for i in range(levels):
        bit = levels - 1 - i
        matrix = tr_ref[first + i]
        origin = x_ref if i == 0 else held
        target = out_ref if i == levels - 1 else held
        for g in range(devices // 2):
            low_at = ((g >> bit) << (bit + 1)) | (g & ((1 << bit) - 1))
            high_at = low_at + (1 << bit)
            rows = gain_ref[half_at + g, 2 * i : 2 * i + 2, :].astype(F32)
            gains = [rows[n : n + 1] for n in range(2)]
            target[low_at], target[high_at] = pair(matrix, origin[low_at], origin[high_at], gains)


def lower_levels(own, x, matrices, gains, first):
    devices, ranks, cols = x.shape
    levels = devices.bit_length() - 1
    return pl.pallas_call(
        functools.partial(lower_kernel, levels, first),
        in_specs=[pl.BlockSpec(memory_space=pltpu.SMEM)] + [pl.BlockSpec(memory_space=pltpu.VMEM)] * 3,
        out_specs=pl.BlockSpec(memory_space=pltpu.VMEM),
        out_shape=jax.ShapeDtypeStruct(x.shape, BF16),
        scratch_shapes=[pltpu.VMEM(x.shape, BF16)],
        compiler_params=params(),
        cost_estimate=cost(levels * devices * cols * 2 * ranks * ranks * 8, devices * ranks * cols * 4),
        name="lower_levels",
    )(own, x, matrices, gains)


def target_kernel(x_ref, map_ref, *refs):
    out_ref = refs[-1]
    pieces, _, _, cols = x_ref.shape
    target_map = map_ref[...]
    for k in range(pieces):
        out_ref[0, :, k * cols : (k + 1) * cols] = dot(target_map, x_ref[k, 0]).astype(BF16)


def to_targets(image, images, x, target_map, pieces, field):
    t_pieces, two, ranks, cols = x.shape
    points = target_map.shape[0]
    per_half = t_pieces // pieces
    operands = [x, target_map] + ([] if field is None else [field])
    return pl.pallas_call(
        target_kernel,
        grid=(two, per_half),
        in_specs=[
            pl.BlockSpec((pieces, 1, ranks, cols), lambda n, i: (i, n, 0, 0)),
            pl.BlockSpec((points, ranks), lambda n, i: (0, 0)),
        ]
        + ([] if field is None else [pl.BlockSpec(memory_space=pl.ANY)]),
        out_specs=pl.BlockSpec((1, points, pieces * cols), lambda n, i: (image, 0, n * per_half + i)),
        out_shape=jax.ShapeDtypeStruct((images, points, two * t_pieces * cols), BF16),
        input_output_aliases={} if field is None else {2: 0},
        compiler_params=params(),
        cost_estimate=cost(points * ranks * two * t_pieces * cols * 4, points * two * t_pieces * cols * 2),
        name="target_map",
    )(*operands)


def body(sources, source_map, translation, box_gain, target_order, target_map):
    images, _, boxes = sources.shape
    ranks = source_map.shape[0]
    n_lower = lax.axis_size("lo")
    matrices = translation.reshape(translation.shape[0], 2 * ranks, 2 * ranks)
    upper = lax.axis_index("hi")
    owns = jnp.stack([upper >> 1 & 1, upper & 1]).astype(jnp.int32)
    first_lower = LOCAL_LEVELS + 2
    levels_lo = n_lower.bit_length() - 1
    piece = boxes // n_lower
    halves = n_lower // 2

    groups = [list(range(halves)), list(range(halves, n_lower))]
    own_half = (lax.axis_index("lo") // halves).astype(jnp.int32).reshape(1)
    gain_rows = -(-2 * levels_lo // 16) * 16

    fronts = [front(c, owns[:1], sources, source_map, matrices, box_gain, 2048) for c in range(images)]
    arrived = []
    for kept, sent in fronts:
        arrived.append(lax.ppermute(sent, "hi", [(i, i ^ 2) for i in range(4)]))
    owns, _ = lax.optimization_barrier((owns, fronts[-1][0]))
    field = None
    for c in range(images):
        kept = fronts[c][0]
        kept, sent = upper_level(LOCAL_LEVELS, owns, kept, arrived[c], matrices, box_gain, 2048)
        received = lax.ppermute(sent, "hi", [(i, i ^ 1) for i in range(4)])
        if c == 0:
            received, arrived[1] = lax.optimization_barrier((received, arrived[1]))
        extra = gain_rows if c == 0 else 0
        x = upper_level(
            LOCAL_LEVELS + 1, owns[1:], kept, received, matrices, box_gain, 2048, n_lower, extra
        )
        x = lax.all_to_all(x.reshape(n_lower, ranks + extra, piece), "lo", 0, 0)
        if c == 0:
            gains = x[:, ranks:, :]
        x = gather(target_order, x, ranks)
        x = lax.all_to_all(x, "lo", 0, 0)
        x = lower_levels(own_half, x, matrices, gains, first_lower)
        x = x.reshape(halves, 2, ranks, piece)
        x = lax.all_to_all(x, "lo", 0, 0, axis_index_groups=groups)
        field = to_targets(c, images, x, target_map, 8, field)
    return field


def solution(mesh):
    return jax.shard_map(
        body,
        mesh=mesh,
        in_specs=(
            P(None, None, ("hi", "lo")),
            P(),
            P(),
            P(None, ("hi", "lo")),
            P(("hi", "lo"), None),
            P(),
        ),
        out_specs=P(None, None, ("hi", "lo")),
        check_vma=False,
    )
```

```python
import functools

import jax
import jax.numpy as jnp
from jax import lax
from jax.experimental import pallas as pl
from jax.experimental.pallas import tpu as pltpu
from jax.sharding import PartitionSpec as P

LOCAL_LEVELS = 8
F32 = jnp.float32
BF16 = jnp.bfloat16
VMEM_LIMIT = 40 * 2**20
FRONT_LIMIT = 56 * 2**20
PARTS = 2


def dot(a, b):
    return jnp.dot(a, b, preferred_element_type=F32)


def params(limit=VMEM_LIMIT):
    return pltpu.CompilerParams(vmem_limit_bytes=limit)


def cost(macs, moved):
    return pl.CostEstimate(flops=2 * macs, bytes_accessed=moved, transcendentals=0)


def pick(own, kept, received):
    first = own == 0
    return jnp.where(first, kept, received), jnp.where(first, received, kept)


def pair(matrix, low, high, gains):
    ranks = low.shape[0]
    product = dot(matrix, jnp.concatenate([low, high], axis=0))
    return (
        (product[:ranks] * gains[0]).astype(BF16),
        (product[ranks:] * gains[1]).astype(BF16),
    )


def front_kernel(levels, own_ref, low_ref, high_ref, map_ref, tr_ref, gl_ref, gh_ref, kept_ref, sent_ref):
    source_map = map_ref[...]
    low = dot(source_map, low_ref[0]).astype(BF16)
    high = dot(source_map, high_ref[0]).astype(BF16)
    for level in range(levels):
        gains = gl_ref[level : level + 1, :], gh_ref[level : level + 1, :]
        low, high = pair(tr_ref[level], low, high, gains)
    kept_ref[...], sent_ref[...] = pick(own_ref[0], low, high)


def front(image, part, parts, own, sources, source_map, matrices, box_gain):
    _, points, boxes = sources.shape
    ranks = source_map.shape[0]
    cols = boxes // 2 // parts
    grid_spec = pltpu.PrefetchScalarGridSpec(
        num_scalar_prefetch=1,
        grid=(1,),
        in_specs=[
            pl.BlockSpec((1, points, cols), lambda i, s: (image, 0, part)),
            pl.BlockSpec((1, points, cols), lambda i, s: (image, 0, parts + part)),
            pl.BlockSpec((ranks, points), lambda i, s: (0, 0)),
            pl.BlockSpec((LOCAL_LEVELS,) + matrices.shape[1:], lambda i, s: (0, 0, 0)),
            pl.BlockSpec((LOCAL_LEVELS, cols), lambda i, s: (0, part)),
            pl.BlockSpec((LOCAL_LEVELS, cols), lambda i, s: (0, parts + part)),
        ],
        out_specs=[pl.BlockSpec((ranks, cols), lambda i, s: (0, 0))] * 2,
    )
    return pl.pallas_call(
        functools.partial(front_kernel, LOCAL_LEVELS),
        grid_spec=grid_spec,
        out_shape=[jax.ShapeDtypeStruct((ranks, cols), BF16)] * 2,
        compiler_params=params(FRONT_LIMIT),
        cost_estimate=cost(2 * cols * ranks * (points + LOCAL_LEVELS * 2 * ranks) * 8, 2 * cols * points * 2),
        name="source_map_and_local_levels",
    )(own, sources, sources, source_map, matrices, box_gain, box_gain)


def swap_kernel(level, own_ref, kept_in, recv_in, tr_ref, gl_ref, gh_ref, kept_ref, sent_ref):
    gains = gl_ref[level : level + 1, :], gh_ref[level : level + 1, :]
    low, high = pick(own_ref[0], kept_in[...], recv_in[...])
    low, high = pair(tr_ref[level], low, high, gains)
    kept_ref[...], sent_ref[...] = pick(own_ref[1], low, high)


def upper_level(level, part, parts, owns, kept, received, matrices, box_gain):
    ranks, cols = kept.shape
    block = pl.BlockSpec((ranks, cols), lambda i, s: (0, 0))
    grid_spec = pltpu.PrefetchScalarGridSpec(
        num_scalar_prefetch=1,
        grid=(1,),
        in_specs=[
            block,
            block,
            pl.BlockSpec(matrices.shape, lambda i, s: (0, 0, 0)),
            pl.BlockSpec((box_gain.shape[0], cols), lambda i, s: (0, part)),
            pl.BlockSpec((box_gain.shape[0], cols), lambda i, s: (0, parts + part)),
        ],
        out_specs=[block] * 2,
    )
    return pl.pallas_call(
        functools.partial(swap_kernel, level),
        grid_spec=grid_spec,
        out_shape=[jax.ShapeDtypeStruct(kept.shape, BF16)] * 2,
        compiler_params=params(),
        cost_estimate=cost(cols * 4 * ranks * ranks * 8, cols * ranks * 8),
        name="upper_level",
    )(owns, kept, received, matrices, box_gain, box_gain)


def rows_kernel(level, images, own_ref, *refs):
    parts, (tr_ref, gl_ref, gh_ref), out_ref = refs[: 2 * images], refs[2 * images : 2 * images + 3], refs[-1]
    gains = gl_ref[level : level + 1, :], gh_ref[level : level + 1, :]
    lows, highs = [], []
    for c in range(images):
        low, high = pick(own_ref[0], parts[c][...], parts[images + c][...])
        low, high = pair(tr_ref[level], low, high, gains)
        lows.append(low)
        highs.append(high)
    piece = gl_ref.shape[1] // out_ref.shape[1]
    width = out_ref.shape[3]
    later = [ref[i : i + 1, :] for i in range(level + 1, gl_ref.shape[0] - 1) for ref in (gl_ref, gh_ref)]
    blank = jnp.zeros((1, width), F32)
    for k in range(out_ref.shape[1]):
        rows = [row[:, at : at + width] for at in range(k * piece, (k + 1) * piece, width) for row in later]
        rows += [blank] * (out_ref.shape[2] - piece - len(rows))
        rows = jnp.concatenate(rows, axis=0).astype(BF16)
        for n in range(2):
            out_ref[n, k, piece:, :] = rows
    for n, blocks in enumerate((lows, highs)):
        stacked = jnp.concatenate(blocks, axis=0).astype(F32)
        for k in range(out_ref.shape[1]):
            out_ref[n, k, :piece, :] = stacked[:, k * piece : (k + 1) * piece].T.astype(BF16)


def rows_level(level, part, parts, owns, kept, received, matrices, box_gain, pieces, extra, before):
    images = len(kept)
    ranks, cols = kept[0].shape
    piece = 2 * parts * cols // pieces
    block = pl.BlockSpec((ranks, cols), lambda i, s: (0, 0))
    more = [] if before is None else [before]
    grid_spec = pltpu.PrefetchScalarGridSpec(
        num_scalar_prefetch=1,
        grid=(1,),
        in_specs=[block] * (2 * images)
        + [
            pl.BlockSpec(matrices.shape, lambda i, s: (0, 0, 0)),
            pl.BlockSpec((box_gain.shape[0], cols), lambda i, s: (0, part)),
            pl.BlockSpec((box_gain.shape[0], cols), lambda i, s: (0, parts + part)),
        ]
        + [pl.BlockSpec(memory_space=pl.ANY)] * len(more),
        out_specs=pl.BlockSpec(
            (2, cols // piece, piece + extra, images * ranks), lambda i, s: (0, part, 0, 0)
        ),
    )
    return pl.pallas_call(
        functools.partial(rows_kernel, level, images),
        grid_spec=grid_spec,
        out_shape=jax.ShapeDtypeStruct((2, pieces // 2, piece + extra, images * ranks), BF16),
        input_output_aliases={2 * images + 4: 0} if more else {},
        compiler_params=params(),
        cost_estimate=cost(images * cols * 4 * ranks * ranks * 8, images * cols * ranks * 8),
        name="upper_level_to_rows",
    )(owns, *kept, *received, matrices, box_gain, box_gain, *more)


UNROLL = 32


def gather_kernel(order_ref, rows_ref, out_ref, table, picked):
    boxes = table.shape[0]
    pieces = rows_ref.shape[0]
    chunk = boxes // pieces

    def widen(i, carry):
        table[pl.ds(pl.multiple_of(i * chunk, chunk), chunk), :] = rows_ref[i, :chunk, :].astype(F32)
        return carry

    lax.fori_loop(0, pieces, widen, 0)

    def move(i, carry):
        base = pl.multiple_of(i * UNROLL, UNROLL)
        for k in range(UNROLL):
            picked[pl.ds(base + k, 1), :] = table[pl.ds(order_ref[0, base + k], 1), :]
        return carry

    lax.fori_loop(0, boxes // UNROLL, move, 0)

    def narrow(i, carry):
        at = pl.ds(pl.multiple_of(i * chunk, chunk), chunk)
        out_ref[at, :] = picked[at, :].astype(BF16)
        return carry

    lax.fori_loop(0, boxes // chunk, narrow, 0)


def gather_rows(order, rows):
    boxes, width = order.shape[1], rows.shape[2]
    return pl.pallas_call(
        gather_kernel,
        in_specs=[
            pl.BlockSpec(memory_space=pltpu.SMEM),
            pl.BlockSpec(memory_space=pltpu.VMEM),
        ],
        out_specs=pl.BlockSpec(memory_space=pltpu.VMEM),
        out_shape=jax.ShapeDtypeStruct((boxes, width), BF16),
        scratch_shapes=[pltpu.VMEM((boxes, width), F32), pltpu.VMEM((boxes, width), F32)],
        compiler_params=params(),
        cost_estimate=cost(0, 30 * 2**20),
        name="box_order",
    )(order, rows)


def lower_kernel(levels, first, own_ref, x_ref, tr_ref, gain_ref, out_ref, held, scales):
    devices, cols, width = x_ref.shape
    images, ranks = out_ref.shape[1], out_ref.shape[2]
    half_at = own_ref[0] * (devices // 2)
    for g in range(devices // 2):
        scales[g] = gain_ref[half_at + g, cols:, :].astype(F32)
    for i in range(levels):
        bit = levels - 1 - i
        matrix = tr_ref[first + i]
        if i == 0:
            blank = jnp.zeros((2 * ranks, ranks), BF16)
            sides = []
            for side in range(2):
                part = matrix[:, side * ranks : (side + 1) * ranks]
                bands = [
                    jnp.concatenate([part if c == b else blank for b in range(images)], axis=1)
                    for c in range(images)
                ]
                sides.append(jnp.concatenate(bands, axis=0))
            both = jnp.concatenate(sides, axis=1)
        target = out_ref if i == levels - 1 else held
        for g in range(devices // 2):
            low_at = ((g >> bit) << (bit + 1)) | (g & ((1 << bit) - 1))
            high_at = low_at + (1 << bit)
            if i < levels - 1:
                gains = []
                for n in range(2):
                    at = [2 * (levels - 1) * k + 2 * i + n for k in range(cols // width)]
                    gains.append(jnp.concatenate([scales[g, r : r + 1, :] for r in at], axis=1))
            if i == 0:
                stacked = jnp.concatenate([x_ref[low_at], x_ref[high_at]], axis=1)
                product = lax.dot_general(
                    both, stacked, (((1,), (1,)), ((), ())), preferred_element_type=F32
                )
            for c in range(images):
                if i == 0:
                    own = product[c * 2 * ranks : (c + 1) * 2 * ranks]
                else:
                    own = dot(matrix, jnp.concatenate([held[low_at, c], held[high_at, c]], axis=0))
                low, high = own[:ranks], own[ranks:]
                if i < levels - 1:
                    low, high = low * gains[0], high * gains[1]
                target[low_at, c] = low.astype(BF16)
                target[high_at, c] = high.astype(BF16)


def lower_levels(own, x, matrices, gains, images, first):
    devices, cols, width = x.shape
    ranks = width // images
    levels = devices.bit_length() - 1
    shape = (devices, images, ranks, cols)
    return pl.pallas_call(
        functools.partial(lower_kernel, levels, first),
        in_specs=[pl.BlockSpec(memory_space=pltpu.SMEM)] + [pl.BlockSpec(memory_space=pltpu.VMEM)] * 3,
        out_specs=pl.BlockSpec(memory_space=pltpu.VMEM),
        out_shape=jax.ShapeDtypeStruct(shape, BF16),
        scratch_shapes=[
            pltpu.VMEM(shape, BF16),
            pltpu.VMEM((devices // 2, gains.shape[1] - cols, width), F32),
        ],
        compiler_params=params(),
        cost_estimate=cost(levels * devices * cols * 2 * width * ranks * 8, devices * width * cols * 4),
        name="lower_levels",
    )(own, x, matrices, gains)


def target_kernel(level, x_ref, map_ref, gain_ref, out_ref):
    pieces, _, images, ranks, cols = x_ref.shape
    target_map = map_ref[...].astype(F32).T.astype(BF16)
    for k in range(pieces):
        at = slice(k * cols, (k + 1) * cols)
        gains = gain_ref[level : level + 1, at]
        for c in range(images):
            scaled = (x_ref[k, 0, c].astype(F32) * gains).astype(BF16)
            out_ref[c, :, at] = dot(target_map, scaled).astype(BF16)


def to_targets(x, target_map, box_gain, pieces):
    t_pieces, two, images, ranks, cols = x.shape
    points = target_map.shape[1]
    per_half = t_pieces // pieces
    return pl.pallas_call(
        functools.partial(target_kernel, box_gain.shape[0] - 1),
        grid=(two, per_half),
        in_specs=[
            pl.BlockSpec((pieces, 1, images, ranks, cols), lambda n, i: (i, n, 0, 0, 0)),
            pl.BlockSpec((ranks, points), lambda n, i: (0, 0)),
            pl.BlockSpec((box_gain.shape[0], pieces * cols), lambda n, i: (0, n * per_half + i)),
        ],
        out_specs=pl.BlockSpec((images, points, pieces * cols), lambda n, i: (0, 0, n * per_half + i)),
        out_shape=jax.ShapeDtypeStruct((images, points, two * t_pieces * cols), BF16),
        compiler_params=params(),
        cost_estimate=cost(images * points * ranks * two * t_pieces * cols * 4, images * points * two * t_pieces * cols * 2),
        name="target_map",
    )(x, target_map, box_gain)


def body(sources, source_map, translation, box_gain, target_order, target_map):
    images, _, boxes = sources.shape
    ranks = source_map.shape[0]
    n_lower = lax.axis_size("lo")
    matrices = translation.reshape(translation.shape[0], 2 * ranks, 2 * ranks)
    upper = lax.axis_index("hi")
    owns = jnp.stack([upper >> 1 & 1, upper & 1]).astype(jnp.int32)
    first_lower = LOCAL_LEVELS + 2
    levels_lo = n_lower.bit_length() - 1
    piece = boxes // n_lower
    halves = n_lower // 2
    groups = [list(range(halves)), list(range(halves, n_lower))]

    own_half = (lax.axis_index("lo") >> levels_lo - 1).astype(jnp.int32).reshape(1)
    extra = -(-2 * (levels_lo - 1) * piece // (images * ranks) // 16) * 16

    kept, received = {}, {}
    for part in range(PARTS):
        for c in range(images):
            at = part, c
            kept[at], sent = front(c, part, PARTS, owns[:1], sources, source_map, matrices, box_gain)
            received[at] = lax.ppermute(sent, "hi", [(i, i ^ 2) for i in range(4)])
    rows = None
    for part in range(PARTS):
        for c in range(images):
            at = part, c
            kept[at], sent = upper_level(
                LOCAL_LEVELS, part, PARTS, owns, kept[at], received[at], matrices, box_gain
            )
            received[at] = lax.ppermute(sent, "hi", [(i, i ^ 1) for i in range(4)])
        rows = rows_level(
            LOCAL_LEVELS + 1,
            part,
            PARTS,
            owns[1:],
            [kept[part, c] for c in range(images)],
            [received[part, c] for c in range(images)],
            matrices,
            box_gain,
            n_lower,
            extra,
            rows,
        )
    own_half, rows = lax.optimization_barrier((own_half, rows))
    moved = lax.all_to_all(rows.reshape(n_lower, piece + extra, images * ranks), "lo", 0, 0)
    rows = gather_rows(target_order, moved)
    rows = lax.all_to_all(rows.reshape(n_lower, piece, images * ranks), "lo", 0, 0)
    blocks = lower_levels(own_half, rows, matrices, moved, images, first_lower)
    blocks = blocks.reshape(halves, 2, images, ranks, piece)
    blocks = lax.all_to_all(blocks, "lo", 0, 0, axis_index_groups=groups)
    return to_targets(blocks, target_map.T, box_gain, 8)


def solution(mesh):
    return jax.shard_map(
        body,
        mesh=mesh,
        in_specs=(
            P(None, None, ("hi", "lo")),
            P(),
            P(),
            P(None, ("hi", "lo")),
            P(("hi", "lo"), None),
            P(),
        ),
        out_specs=P(None, None, ("hi", "lo")),
        check_vma=False,
    )
```

```python
import functools

import jax
import jax.numpy as jnp
from jax import lax
from jax.experimental import pallas as pl
from jax.experimental.pallas import tpu as pltpu
from jax.sharding import PartitionSpec as P

LOCAL_LEVELS = 8
F32 = jnp.float32
BF16 = jnp.bfloat16
VMEM_LIMIT = 40 * 2**20
FRONT_LIMIT = 56 * 2**20
PARTS = 2
TURN_STEPS = 2


def dot(a, b):
    return jnp.dot(a, b, preferred_element_type=F32)


def params(limit=VMEM_LIMIT):
    return pltpu.CompilerParams(vmem_limit_bytes=limit)


def cost(macs, moved):
    return pl.CostEstimate(flops=2 * macs, bytes_accessed=moved, transcendentals=0)


def pick(own, kept, received):
    first = own == 0
    return jnp.where(first, kept, received), jnp.where(first, received, kept)


def pair(matrix, low, high, gains):
    ranks = low.shape[0]
    product = dot(matrix, jnp.concatenate([low, high], axis=0))
    return (
        (product[:ranks] * gains[0]).astype(BF16),
        (product[ranks:] * gains[1]).astype(BF16),
    )


def front_kernel(levels, own_ref, low_ref, high_ref, map_ref, tr_ref, gl_ref, gh_ref, kept_ref, sent_ref):
    source_map = map_ref[...]
    low = dot(source_map, low_ref[0]).astype(BF16)
    high = dot(source_map, high_ref[0]).astype(BF16)
    for level in range(levels):
        gains = gl_ref[level : level + 1, :], gh_ref[level : level + 1, :]
        low, high = pair(tr_ref[level], low, high, gains)
    kept_ref[...], sent_ref[...] = pick(own_ref[0], low, high)


def front(image, part, parts, own, sources, source_map, matrices, box_gain):
    _, points, boxes = sources.shape
    ranks = source_map.shape[0]
    cols = boxes // 2 // parts
    grid_spec = pltpu.PrefetchScalarGridSpec(
        num_scalar_prefetch=1,
        grid=(1,),
        in_specs=[
            pl.BlockSpec((1, points, cols), lambda i, s: (image, 0, part)),
            pl.BlockSpec((1, points, cols), lambda i, s: (image, 0, parts + part)),
            pl.BlockSpec((ranks, points), lambda i, s: (0, 0)),
            pl.BlockSpec((LOCAL_LEVELS,) + matrices.shape[1:], lambda i, s: (0, 0, 0)),
            pl.BlockSpec((LOCAL_LEVELS, cols), lambda i, s: (0, part)),
            pl.BlockSpec((LOCAL_LEVELS, cols), lambda i, s: (0, parts + part)),
        ],
        out_specs=[pl.BlockSpec((ranks, cols), lambda i, s: (0, 0))] * 2,
    )
    return pl.pallas_call(
        functools.partial(front_kernel, LOCAL_LEVELS),
        grid_spec=grid_spec,
        out_shape=[jax.ShapeDtypeStruct((ranks, cols), BF16)] * 2,
        compiler_params=params(FRONT_LIMIT),
        cost_estimate=cost(2 * cols * ranks * (points + LOCAL_LEVELS * 2 * ranks) * 8, 2 * cols * points * 2),
        name="source_map_and_local_levels",
    )(own, sources, sources, source_map, matrices, box_gain, box_gain)


def swap_kernel(level, own_ref, kept_in, recv_in, tr_ref, gl_ref, gh_ref, kept_ref, sent_ref):
    gains = gl_ref[level : level + 1, :], gh_ref[level : level + 1, :]
    low, high = pick(own_ref[0], kept_in[...], recv_in[...])
    low, high = pair(tr_ref[level], low, high, gains)
    kept_ref[...], sent_ref[...] = pick(own_ref[1], low, high)


def upper_level(level, part, parts, owns, kept, received, matrices, box_gain):
    ranks, cols = kept.shape
    block = pl.BlockSpec((ranks, cols), lambda i, s: (0, 0))
    grid_spec = pltpu.PrefetchScalarGridSpec(
        num_scalar_prefetch=1,
        grid=(1,),
        in_specs=[
            block,
            block,
            pl.BlockSpec(matrices.shape, lambda i, s: (0, 0, 0)),
            pl.BlockSpec((box_gain.shape[0], cols), lambda i, s: (0, part)),
            pl.BlockSpec((box_gain.shape[0], cols), lambda i, s: (0, parts + part)),
        ],
        out_specs=[block] * 2,
    )
    return pl.pallas_call(
        functools.partial(swap_kernel, level),
        grid_spec=grid_spec,
        out_shape=[jax.ShapeDtypeStruct(kept.shape, BF16)] * 2,
        compiler_params=params(),
        cost_estimate=cost(cols * 4 * ranks * ranks * 8, cols * ranks * 8),
        name="upper_level",
    )(owns, kept, received, matrices, box_gain, box_gain)


def rows_kernel(level, images, own_ref, *refs):
    parts, (tr_ref, gl_ref, gh_ref), out_ref = refs[: 2 * images], refs[2 * images : 2 * images + 3], refs[-1]
    gains = gl_ref[level : level + 1, :], gh_ref[level : level + 1, :]
    lows, highs = [], []
    for c in range(images):
        low, high = pick(own_ref[0], parts[c][...], parts[images + c][...])
        low, high = pair(tr_ref[level], low, high, gains)
        lows.append(low)
        highs.append(high)
    piece = gl_ref.shape[1] // out_ref.shape[1]
    width = out_ref.shape[3]
    later = [ref[i : i + 1, :] for i in range(level + 1, gl_ref.shape[0] - 1) for ref in (gl_ref, gh_ref)]
    blank = jnp.zeros((1, width), F32)
    for k in range(out_ref.shape[1]):
        rows = [row[:, at : at + width] for at in range(k * piece, (k + 1) * piece, width) for row in later]
        rows += [blank] * (out_ref.shape[2] - piece - len(rows))
        rows = jnp.concatenate(rows, axis=0).astype(BF16)
        for n in range(2):
            out_ref[n, k, piece:, :] = rows
    for n, blocks in enumerate((lows, highs)):
        stacked = jnp.concatenate(blocks, axis=0).astype(F32)
        for k in range(out_ref.shape[1]):
            out_ref[n, k, :piece, :] = stacked[:, k * piece : (k + 1) * piece].T.astype(BF16)


def rows_level(level, part, parts, owns, kept, received, matrices, box_gain, pieces, extra, before):
    images = len(kept)
    ranks, cols = kept[0].shape
    piece = 2 * parts * cols // pieces
    block = pl.BlockSpec((ranks, cols), lambda i, s: (0, 0))
    more = [] if before is None else [before]
    grid_spec = pltpu.PrefetchScalarGridSpec(
        num_scalar_prefetch=1,
        grid=(1,),
        in_specs=[block] * (2 * images)
        + [
            pl.BlockSpec(matrices.shape, lambda i, s: (0, 0, 0)),
            pl.BlockSpec((box_gain.shape[0], cols), lambda i, s: (0, part)),
            pl.BlockSpec((box_gain.shape[0], cols), lambda i, s: (0, parts + part)),
        ]
        + [pl.BlockSpec(memory_space=pl.ANY)] * len(more),
        out_specs=pl.BlockSpec(
            (2, cols // piece, piece + extra, images * ranks), lambda i, s: (0, part, 0, 0)
        ),
    )
    return pl.pallas_call(
        functools.partial(rows_kernel, level, images),
        grid_spec=grid_spec,
        out_shape=jax.ShapeDtypeStruct((2, pieces // 2, piece + extra, images * ranks), BF16),
        input_output_aliases={2 * images + 4: 0} if more else {},
        compiler_params=params(),
        cost_estimate=cost(images * cols * 4 * ranks * ranks * 8, images * cols * ranks * 8),
        name="upper_level_to_rows",
    )(owns, *kept, *received, matrices, box_gain, box_gain, *more)


UNROLL = 128


def gather_kernel(order_ref, rows_ref, out_ref, table, picked):
    boxes = table.shape[0]
    pieces = rows_ref.shape[0]
    chunk = boxes // pieces

    def widen(i, carry):
        table[pl.ds(pl.multiple_of(i * chunk, chunk), chunk), :] = rows_ref[i, :chunk, :].astype(F32)
        return carry

    lax.fori_loop(0, pieces, widen, 0)

    def move(i, carry):
        base = pl.multiple_of(i * UNROLL, UNROLL)
        for k in range(UNROLL):
            picked[pl.ds(base + k, 1), :] = table[pl.ds(order_ref[0, base + k], 1), :]
        return carry

    lax.fori_loop(0, boxes // UNROLL, move, 0)

    def narrow(i, carry):
        at = pl.ds(pl.multiple_of(i * chunk, chunk), chunk)
        out_ref[at, :] = picked[at, :].astype(BF16)
        return carry

    lax.fori_loop(0, boxes // chunk, narrow, 0)


def gather_rows(order, rows):
    boxes, width = order.shape[1], rows.shape[2]
    return pl.pallas_call(
        gather_kernel,
        in_specs=[
            pl.BlockSpec(memory_space=pltpu.SMEM),
            pl.BlockSpec(memory_space=pltpu.VMEM),
        ],
        out_specs=pl.BlockSpec(memory_space=pltpu.VMEM),
        out_shape=jax.ShapeDtypeStruct((boxes, width), BF16),
        scratch_shapes=[pltpu.VMEM((boxes, width), F32), pltpu.VMEM((boxes, width), F32)],
        compiler_params=params(),
        cost_estimate=cost(0, 30 * 2**20),
        name="box_order",
    )(order, rows)


def lower_kernel(levels, first, own_ref, x_ref, tr_ref, gain_ref, out_ref, held, scales):
    devices, cols, width = x_ref.shape
    images, ranks = out_ref.shape[1], out_ref.shape[2]
    half_at = own_ref[0] * (devices // 2)
    for g in range(devices // 2):
        scales[g] = gain_ref[half_at + g, cols:, :].astype(F32)
    for i in range(levels):
        bit = levels - 1 - i
        matrix = tr_ref[first + i]
        if i == 0:
            blank = jnp.zeros((2 * ranks, ranks), BF16)
            sides = []
            for side in range(2):
                part = matrix[:, side * ranks : (side + 1) * ranks]
                bands = [
                    jnp.concatenate([part if c == b else blank for b in range(images)], axis=1)
                    for c in range(images)
                ]
                sides.append(jnp.concatenate(bands, axis=0))
            both = jnp.concatenate(sides, axis=1)
        target = out_ref if i == levels - 1 else held
        for g in range(devices // 2):
            low_at = ((g >> bit) << (bit + 1)) | (g & ((1 << bit) - 1))
            high_at = low_at + (1 << bit)
            if i < levels - 1:
                gains = []
                for n in range(2):
                    at = [2 * (levels - 1) * k + 2 * i + n for k in range(cols // width)]
                    gains.append(jnp.concatenate([scales[g, r : r + 1, :] for r in at], axis=1))
            if i == 0:
                stacked = jnp.concatenate([x_ref[low_at], x_ref[high_at]], axis=1)
                product = lax.dot_general(
                    both, stacked, (((1,), (1,)), ((), ())), preferred_element_type=F32
                )
            for c in range(images):
                if i == 0:
                    own = product[c * 2 * ranks : (c + 1) * 2 * ranks]
                else:
                    own = dot(matrix, jnp.concatenate([held[low_at, c], held[high_at, c]], axis=0))
                low, high = own[:ranks], own[ranks:]
                if i < levels - 1:
                    low, high = low * gains[0], high * gains[1]
                target[low_at, c] = low.astype(BF16)
                target[high_at, c] = high.astype(BF16)


def lower_levels(own, x, matrices, gains, images, first):
    devices, cols, width = x.shape
    ranks = width // images
    levels = devices.bit_length() - 1
    shape = (devices, images, ranks, cols)
    return pl.pallas_call(
        functools.partial(lower_kernel, levels, first),
        in_specs=[pl.BlockSpec(memory_space=pltpu.SMEM)] + [pl.BlockSpec(memory_space=pltpu.VMEM)] * 3,
        out_specs=pl.BlockSpec(memory_space=pltpu.VMEM),
        out_shape=jax.ShapeDtypeStruct(shape, BF16),
        scratch_shapes=[
            pltpu.VMEM(shape, BF16),
            pltpu.VMEM((devices // 2, gains.shape[1] - cols, width), F32),
        ],
        compiler_params=params(),
        cost_estimate=cost(levels * devices * cols * 2 * width * ranks * 8, devices * width * cols * 4),
        name="lower_levels",
    )(own, x, matrices, gains)


def target_kernel(level, x_ref, map_ref, gain_ref, out_ref):
    pieces, _, images, ranks, cols = x_ref.shape
    target_map = map_ref[...].astype(F32).T.astype(BF16)
    for k in range(pieces):
        at = slice(k * cols, (k + 1) * cols)
        gains = gain_ref[level : level + 1, at]
        for c in range(images):
            scaled = (x_ref[k, 0, c].astype(F32) * gains).astype(BF16)
            out_ref[c, :, at] = dot(target_map, scaled).astype(BF16)


def to_targets(x, target_map, box_gain, pieces):
    t_pieces, two, images, ranks, cols = x.shape
    points = target_map.shape[1]
    per_half = t_pieces // pieces
    return pl.pallas_call(
        functools.partial(target_kernel, box_gain.shape[0] - 1),
        grid=(two, per_half),
        in_specs=[
            pl.BlockSpec((pieces, 1, images, ranks, cols), lambda n, i: (i, n, 0, 0, 0)),
            pl.BlockSpec((ranks, points), lambda n, i: (0, 0)),
            pl.BlockSpec((box_gain.shape[0], pieces * cols), lambda n, i: (0, n * per_half + i)),
        ],
        out_specs=pl.BlockSpec((images, points, pieces * cols), lambda n, i: (0, 0, n * per_half + i)),
        out_shape=jax.ShapeDtypeStruct((images, points, two * t_pieces * cols), BF16),
        compiler_params=params(),
        cost_estimate=cost(images * points * ranks * two * t_pieces * cols * 4, images * points * two * t_pieces * cols * 2),
        name="target_map",
    )(x, target_map, box_gain)


def body(sources, source_map, translation, box_gain, target_order, target_map):
    images, _, boxes = sources.shape
    ranks = source_map.shape[0]
    n_lower = lax.axis_size("lo")
    matrices = translation.reshape(translation.shape[0], 2 * ranks, 2 * ranks)
    upper = lax.axis_index("hi")
    owns = jnp.stack([upper >> 1 & 1, upper & 1]).astype(jnp.int32)
    first_lower = LOCAL_LEVELS + 2
    levels_lo = n_lower.bit_length() - 1
    piece = boxes // n_lower
    halves = n_lower // 2
    groups = [list(range(halves)), list(range(halves, n_lower))]

    own_half = (lax.axis_index("lo") >> levels_lo - 1).astype(jnp.int32).reshape(1)
    extra = -(-2 * (levels_lo - 1) * piece // (images * ranks) // 16) * 16

    kept, received = {}, {}
    for part in range(PARTS):
        for c in range(images):
            at = part, c
            kept[at], sent = front(c, part, PARTS, owns[:1], sources, source_map, matrices, box_gain)
            received[at] = lax.ppermute(sent, "hi", [(i, i ^ 2) for i in range(4)])
    rows, turn = None, own_half
    for part in range(PARTS):
        for c in range(images):
            at = part, c
            kept[at], sent = upper_level(
                LOCAL_LEVELS, part, PARTS, owns, kept[at], received[at], matrices, box_gain
            )
            turn, sent = lax.optimization_barrier((turn, sent))
            received[at] = lax.ppermute(sent, "hi", [(i, i ^ 1) for i in range(4)])
        rows = rows_level(
            LOCAL_LEVELS + 1,
            part,
            PARTS,
            owns[1:],
            [kept[part, c] for c in range(images)],
            [received[part, c] for c in range(images)],
            matrices,
            box_gain,
            n_lower,
            extra,
            rows,
        )
    for _ in range(TURN_STEPS):
        turn = lax.ppermute(turn, "hi", [(1, 3), (3, 1)])
    own_half, rows = lax.optimization_barrier((jnp.where(owns[1:] == 0, own_half, turn), rows))
    moved = lax.all_to_all(rows.reshape(n_lower, piece + extra, images * ranks), "lo", 0, 0)
    rows = gather_rows(target_order, moved)
    rows = lax.all_to_all(rows.reshape(n_lower, piece, images * ranks), "lo", 0, 0)
    blocks = lower_levels(own_half, rows, matrices, moved, images, first_lower)
    blocks = blocks.reshape(halves, 2, images, ranks, piece)
    blocks = lax.all_to_all(blocks, "lo", 0, 0, axis_index_groups=groups)
    return to_targets(blocks, target_map.T, box_gain, 8)


def solution(mesh):
    return jax.shard_map(
        body,
        mesh=mesh,
        in_specs=(
            P(None, None, ("hi", "lo")),
            P(),
            P(),
            P(None, ("hi", "lo")),
            P(("hi", "lo"), None),
            P(),
        ),
        out_specs=P(None, None, ("hi", "lo")),
        check_vma=False,
    )
```

```python
import functools

import jax
import jax.numpy as jnp
from jax import lax
from jax.experimental import pallas as pl
from jax.experimental.pallas import tpu as pltpu
from jax.sharding import PartitionSpec as P

LOCAL_LEVELS = 8
F32 = jnp.float32
BF16 = jnp.bfloat16
VMEM_LIMIT = 40 * 2**20
FRONT_LIMIT = 56 * 2**20
PARTS = 1
TURN_STEPS = 2
PARTNER = 66


def dot(a, b):
    return jnp.dot(a, b, preferred_element_type=F32)


def params(limit=VMEM_LIMIT):
    return pltpu.CompilerParams(vmem_limit_bytes=limit)


def cost(macs, moved):
    return pl.CostEstimate(flops=2 * macs, bytes_accessed=moved, transcendentals=0)


def pick(own, kept, received):
    first = own == 0
    return jnp.where(first, kept, received), jnp.where(first, received, kept)


def pair(matrix, low, high, gains):
    ranks = low.shape[0]
    product = dot(matrix, jnp.concatenate([low, high], axis=0))
    return (
        (product[:ranks] * gains[0]).astype(BF16),
        (product[ranks:] * gains[1]).astype(BF16),
    )


def front_kernel(levels, own_ref, low_ref, high_ref, map_ref, tr_ref, gl_ref, gh_ref, kept_ref, sent_ref):
    source_map = map_ref[...]
    low = dot(source_map, low_ref[0]).astype(BF16)
    high = dot(source_map, high_ref[0]).astype(BF16)
    for level in range(levels):
        gains = gl_ref[level : level + 1, :], gh_ref[level : level + 1, :]
        low, high = pair(tr_ref[level], low, high, gains)
    kept_ref[...], sent_ref[...] = pick(own_ref[0], low, high)


def front(image, part, parts, own, sources, source_map, matrices, box_gain):
    _, points, boxes = sources.shape
    ranks = source_map.shape[0]
    cols = boxes // 2 // parts
    grid_spec = pltpu.PrefetchScalarGridSpec(
        num_scalar_prefetch=1,
        grid=(1,),
        in_specs=[
            pl.BlockSpec((1, points, cols), lambda i, s: (image, 0, part)),
            pl.BlockSpec((1, points, cols), lambda i, s: (image, 0, parts + part)),
            pl.BlockSpec((ranks, points), lambda i, s: (0, 0)),
            pl.BlockSpec((LOCAL_LEVELS,) + matrices.shape[1:], lambda i, s: (0, 0, 0)),
            pl.BlockSpec((LOCAL_LEVELS, cols), lambda i, s: (0, part)),
            pl.BlockSpec((LOCAL_LEVELS, cols), lambda i, s: (0, parts + part)),
        ],
        out_specs=[pl.BlockSpec((ranks, cols), lambda i, s: (0, 0))] * 2,
    )
    return pl.pallas_call(
        functools.partial(front_kernel, LOCAL_LEVELS),
        grid_spec=grid_spec,
        out_shape=[jax.ShapeDtypeStruct((ranks, cols), BF16)] * 2,
        compiler_params=params(FRONT_LIMIT),
        cost_estimate=cost(2 * cols * ranks * (points + LOCAL_LEVELS * 2 * ranks) * 8, 2 * cols * points * 2),
        name="source_map_and_local_levels",
    )(own, sources, sources, source_map, matrices, box_gain, box_gain)


def swap_kernel(level, own_ref, kept_in, recv_in, tr_ref, gl_ref, gh_ref, kept_ref, sent_ref):
    gains = gl_ref[level : level + 1, :], gh_ref[level : level + 1, :]
    low, high = pick(own_ref[0], kept_in[...], recv_in[...])
    low, high = pair(tr_ref[level], low, high, gains)
    kept_ref[...], sent_ref[...] = pick(own_ref[1], low, high)


def upper_level(level, part, parts, owns, kept, received, matrices, box_gain):
    ranks, cols = kept.shape
    block = pl.BlockSpec((ranks, cols), lambda i, s: (0, 0))
    grid_spec = pltpu.PrefetchScalarGridSpec(
        num_scalar_prefetch=1,
        grid=(1,),
        in_specs=[
            block,
            block,
            pl.BlockSpec(matrices.shape, lambda i, s: (0, 0, 0)),
            pl.BlockSpec((box_gain.shape[0], cols), lambda i, s: (0, part)),
            pl.BlockSpec((box_gain.shape[0], cols), lambda i, s: (0, parts + part)),
        ],
        out_specs=[block] * 2,
    )
    return pl.pallas_call(
        functools.partial(swap_kernel, level),
        grid_spec=grid_spec,
        out_shape=[jax.ShapeDtypeStruct(kept.shape, BF16)] * 2,
        compiler_params=params(),
        cost_estimate=cost(cols * 4 * ranks * ranks * 8, cols * ranks * 8),
        name="upper_level",
    )(owns, kept, received, matrices, box_gain, box_gain)


def rows_kernel(level, images, own_ref, *refs):
    parts, (tr_ref, gl_ref, gh_ref), out_ref = refs[: 2 * images], refs[2 * images : 2 * images + 3], refs[-1]
    gains = gl_ref[level : level + 1, :], gh_ref[level : level + 1, :]
    lows, highs = [], []
    for c in range(images):
        low, high = pick(own_ref[0], parts[c][...], parts[images + c][...])
        low, high = pair(tr_ref[level], low, high, gains)
        lows.append(low)
        highs.append(high)
    piece = gl_ref.shape[1] // out_ref.shape[1]
    width = out_ref.shape[3]
    later = [ref[i : i + 1, :] for i in range(level + 1, gl_ref.shape[0] - 1) for ref in (gl_ref, gh_ref)]
    blank = jnp.zeros((1, width), F32)
    for k in range(out_ref.shape[1]):
        rows = [row[:, at : at + width] for at in range(k * piece, (k + 1) * piece, width) for row in later]
        rows += [blank] * (out_ref.shape[2] - piece - len(rows))
        rows = jnp.concatenate(rows, axis=0).astype(BF16)
        for n in range(2):
            out_ref[n, k, piece:, :] = rows
    for n, blocks in enumerate((lows, highs)):
        stacked = jnp.concatenate(blocks, axis=0).astype(F32)
        for k in range(out_ref.shape[1]):
            out_ref[n, k, :piece, :] = stacked[:, k * piece : (k + 1) * piece].T.astype(BF16)


def rows_level(level, part, parts, owns, kept, received, matrices, box_gain, pieces, extra, before):
    images = len(kept)
    ranks, cols = kept[0].shape
    piece = 2 * parts * cols // pieces
    block = pl.BlockSpec((ranks, cols), lambda i, s: (0, 0))
    more = [] if before is None else [before]
    grid_spec = pltpu.PrefetchScalarGridSpec(
        num_scalar_prefetch=1,
        grid=(1,),
        in_specs=[block] * (2 * images)
        + [
            pl.BlockSpec(matrices.shape, lambda i, s: (0, 0, 0)),
            pl.BlockSpec((box_gain.shape[0], cols), lambda i, s: (0, part)),
            pl.BlockSpec((box_gain.shape[0], cols), lambda i, s: (0, parts + part)),
        ]
        + [pl.BlockSpec(memory_space=pl.ANY)] * len(more),
        out_specs=pl.BlockSpec(
            (2, cols // piece, piece + extra, images * ranks), lambda i, s: (0, part, 0, 0)
        ),
    )
    return pl.pallas_call(
        functools.partial(rows_kernel, level, images),
        grid_spec=grid_spec,
        out_shape=jax.ShapeDtypeStruct((2, pieces // 2, piece + extra, images * ranks), BF16),
        input_output_aliases={2 * images + 4: 0} if more else {},
        compiler_params=params(),
        cost_estimate=cost(images * cols * 4 * ranks * ranks * 8, images * cols * ranks * 8),
        name="upper_level_to_rows",
    )(owns, *kept, *received, matrices, box_gain, box_gain, *more)


UNROLL = 128


def gather_kernel(order_ref, rows_ref, out_ref, table, picked):
    boxes = table.shape[0]
    pieces = rows_ref.shape[0]
    chunk = boxes // pieces

    def widen(i, carry):
        table[pl.ds(pl.multiple_of(i * chunk, chunk), chunk), :] = rows_ref[i, :chunk, :].astype(F32)
        return carry

    lax.fori_loop(0, pieces, widen, 0)

    def move(i, carry):
        base = pl.multiple_of(i * UNROLL, UNROLL)
        for k in range(UNROLL):
            picked[pl.ds(base + k, 1), :] = table[pl.ds(order_ref[0, base + k], 1), :]
        return carry

    lax.fori_loop(0, boxes // UNROLL, move, 0)

    def narrow(i, carry):
        at = pl.ds(pl.multiple_of(i * chunk, chunk), chunk)
        out_ref[at, :] = picked[at, :].astype(BF16)
        return carry

    lax.fori_loop(0, boxes // chunk, narrow, 0)


def gather_rows(order, rows):
    boxes, width = order.shape[1], rows.shape[2]
    return pl.pallas_call(
        gather_kernel,
        in_specs=[
            pl.BlockSpec(memory_space=pltpu.SMEM),
            pl.BlockSpec(memory_space=pltpu.VMEM),
        ],
        out_specs=pl.BlockSpec(memory_space=pltpu.VMEM),
        out_shape=jax.ShapeDtypeStruct((boxes, width), BF16),
        scratch_shapes=[pltpu.VMEM((boxes, width), F32), pltpu.VMEM((boxes, width), F32)],
        compiler_params=params(),
        cost_estimate=cost(0, 30 * 2**20),
        name="box_order",
    )(order, rows)


def lower_kernel(levels, first, own_ref, x_ref, tr_ref, gain_ref, out_ref, held, scales):
    devices, cols, width = x_ref.shape
    images, ranks = out_ref.shape[1], out_ref.shape[2]
    half_at = own_ref[0] * (devices // 2)
    for g in range(devices // 2):
        scales[g] = gain_ref[half_at + g, cols:, :].astype(F32)
    for i in range(levels):
        bit = levels - 1 - i
        matrix = tr_ref[first + i]
        if i == 0:
            blank = jnp.zeros((2 * ranks, ranks), BF16)
            sides = []
            for side in range(2):
                part = matrix[:, side * ranks : (side + 1) * ranks]
                bands = [
                    jnp.concatenate([part if c == b else blank for b in range(images)], axis=1)
                    for c in range(images)
                ]
                sides.append(jnp.concatenate(bands, axis=0))
            both = jnp.concatenate(sides, axis=1)
        target = out_ref if i == levels - 1 else held
        for g in range(devices // 2):
            low_at = ((g >> bit) << (bit + 1)) | (g & ((1 << bit) - 1))
            high_at = low_at + (1 << bit)
            if i < levels - 1:
                gains = []
                for n in range(2):
                    at = [2 * (levels - 1) * k + 2 * i + n for k in range(cols // width)]
                    gains.append(jnp.concatenate([scales[g, r : r + 1, :] for r in at], axis=1))
            if i == 0:
                stacked = jnp.concatenate([x_ref[low_at], x_ref[high_at]], axis=1)
                product = lax.dot_general(
                    both, stacked, (((1,), (1,)), ((), ())), preferred_element_type=F32
                )
            for c in range(images):
                if i == 0:
                    own = product[c * 2 * ranks : (c + 1) * 2 * ranks]
                else:
                    own = dot(matrix, jnp.concatenate([held[low_at, c], held[high_at, c]], axis=0))
                low, high = own[:ranks], own[ranks:]
                if i < levels - 1:
                    low, high = low * gains[0], high * gains[1]
                target[low_at, c] = low.astype(BF16)
                target[high_at, c] = high.astype(BF16)


def lower_levels(own, x, matrices, gains, images, first):
    devices, cols, width = x.shape
    ranks = width // images
    levels = devices.bit_length() - 1
    shape = (devices, images, ranks, cols)
    return pl.pallas_call(
        functools.partial(lower_kernel, levels, first),
        in_specs=[pl.BlockSpec(memory_space=pltpu.SMEM)] + [pl.BlockSpec(memory_space=pltpu.VMEM)] * 3,
        out_specs=pl.BlockSpec(memory_space=pltpu.VMEM),
        out_shape=jax.ShapeDtypeStruct(shape, BF16),
        scratch_shapes=[
            pltpu.VMEM(shape, BF16),
            pltpu.VMEM((devices // 2, gains.shape[1] - cols, width), F32),
        ],
        compiler_params=params(),
        cost_estimate=cost(levels * devices * cols * 2 * width * ranks * 8, devices * width * cols * 4),
        name="lower_levels",
    )(own, x, matrices, gains)


def target_kernel(level, x_ref, map_ref, gain_ref, out_ref):
    pieces, _, images, ranks, cols = x_ref.shape
    target_map = map_ref[...].astype(F32).T.astype(BF16)
    for k in range(pieces):
        at = slice(k * cols, (k + 1) * cols)
        gains = gain_ref[level : level + 1, at]
        for c in range(images):
            scaled = (x_ref[k, 0, c].astype(F32) * gains).astype(BF16)
            out_ref[c, :, at] = dot(target_map, scaled).astype(BF16)


def to_targets(x, target_map, box_gain, pieces):
    t_pieces, two, images, ranks, cols = x.shape
    points = target_map.shape[1]
    per_half = t_pieces // pieces
    return pl.pallas_call(
        functools.partial(target_kernel, box_gain.shape[0] - 1),
        grid=(two, per_half),
        in_specs=[
            pl.BlockSpec((pieces, 1, images, ranks, cols), lambda n, i: (i, n, 0, 0, 0)),
            pl.BlockSpec((ranks, points), lambda n, i: (0, 0)),
            pl.BlockSpec((box_gain.shape[0], pieces * cols), lambda n, i: (0, n * per_half + i)),
        ],
        out_specs=pl.BlockSpec((images, points, pieces * cols), lambda n, i: (0, 0, n * per_half + i)),
        out_shape=jax.ShapeDtypeStruct((images, points, two * t_pieces * cols), BF16),
        compiler_params=params(),
        cost_estimate=cost(images * points * ranks * two * t_pieces * cols * 4, images * points * two * t_pieces * cols * 2),
        name="target_map",
    )(x, target_map, box_gain)


def body(sources, source_map, translation, box_gain, target_order, target_map):
    images, _, boxes = sources.shape
    ranks = source_map.shape[0]
    n_lower = lax.axis_size("lo")
    matrices = translation.reshape(translation.shape[0], 2 * ranks, 2 * ranks)
    upper = lax.axis_index("hi")
    owns = jnp.stack([upper >> 1 & 1, upper & 1]).astype(jnp.int32)
    first_lower = LOCAL_LEVELS + 2
    levels_lo = n_lower.bit_length() - 1
    piece = boxes // n_lower
    halves = n_lower // 2
    groups = [list(range(halves)), list(range(halves, n_lower))]

    own_half = (lax.axis_index("lo") >> levels_lo - 1).astype(jnp.int32).reshape(1)
    extra = -(-2 * (levels_lo - 1) * piece // (images * ranks) // 16) * 16

    kept, received = {}, {}
    for part in range(PARTS):
        for c in range(images):
            at = part, c
            kept[at], sent = front(c, part, PARTS, owns[:1], sources, source_map, matrices, box_gain)
            received[at] = lax.ppermute(sent, "hi", [(i, i ^ 2) for i in range(4)])
    rows, turn = None, own_half
    for part in range(PARTS):
        for c in range(images):
            at = part, c
            kept[at], sent = upper_level(
                LOCAL_LEVELS, part, PARTS, owns, kept[at], received[at], matrices, box_gain
            )
            turn, sent = lax.optimization_barrier((turn, sent))
            received[at] = lax.ppermute(sent, "hi", [(i, i ^ 1) for i in range(4)])
        rows = rows_level(
            LOCAL_LEVELS + 1,
            part,
            PARTS,
            owns[1:],
            [kept[part, c] for c in range(images)],
            [received[part, c] for c in range(images)],
            matrices,
            box_gain,
            n_lower,
            extra,
            rows,
        )
    over_zx = [(d, d ^ PARTNER) for d in range(4 * n_lower) if d & n_lower]
    for _ in range(TURN_STEPS):
        turn = lax.ppermute(turn, ("hi", "lo"), over_zx)
    own_half, rows = lax.optimization_barrier((jnp.where(owns[1:] == 0, own_half, turn), rows))
    moved = lax.all_to_all(rows.reshape(n_lower, piece + extra, images * ranks), "lo", 0, 0)
    rows = gather_rows(target_order, moved)
    rows = lax.all_to_all(rows.reshape(n_lower, piece, images * ranks), "lo", 0, 0)
    blocks = lower_levels(own_half, rows, matrices, moved, images, first_lower)
    blocks = blocks.reshape(halves, 2, images, ranks, piece)
    blocks = lax.all_to_all(blocks, "lo", 0, 0, axis_index_groups=groups)
    return to_targets(blocks, target_map.T, box_gain, 8)


def solution(mesh):
    return jax.shard_map(
        body,
        mesh=mesh,
        in_specs=(
            P(None, None, ("hi", "lo")),
            P(),
            P(),
            P(None, ("hi", "lo")),
            P(("hi", "lo"), None),
            P(),
        ),
        out_specs=P(None, None, ("hi", "lo")),
        check_vma=False,
    )
```

```python
import functools

import jax
import jax.numpy as jnp
from jax import lax
from jax.experimental import pallas as pl
from jax.experimental.pallas import tpu as pltpu
from jax.sharding import PartitionSpec as P

LOCAL_LEVELS = 8
F32 = jnp.float32
BF16 = jnp.bfloat16
VMEM_LIMIT = 40 * 2**20
FRONT_LIMIT = 56 * 2**20
PARTS = 1
PARTNERS = 74, 66


def dot(a, b):
    return jnp.dot(a, b, preferred_element_type=F32)


def params(limit=VMEM_LIMIT):
    return pltpu.CompilerParams(vmem_limit_bytes=limit)


def cost(macs, moved):
    return pl.CostEstimate(flops=2 * macs, bytes_accessed=moved, transcendentals=0)


def pick(own, kept, received):
    first = own == 0
    return jnp.where(first, kept, received), jnp.where(first, received, kept)


def pair(matrix, low, high, gains):
    ranks = low.shape[0]
    product = dot(matrix, jnp.concatenate([low, high], axis=0))
    return (
        (product[:ranks] * gains[0]).astype(BF16),
        (product[ranks:] * gains[1]).astype(BF16),
    )


def front_kernel(levels, own_ref, low_ref, high_ref, map_ref, tr_ref, gl_ref, gh_ref, kept_ref, sent_ref):
    source_map = map_ref[...]
    low = dot(source_map, low_ref[0]).astype(BF16)
    high = dot(source_map, high_ref[0]).astype(BF16)
    for level in range(levels):
        gains = gl_ref[level : level + 1, :], gh_ref[level : level + 1, :]
        low, high = pair(tr_ref[level], low, high, gains)
    kept_ref[...], sent_ref[...] = pick(own_ref[0], low, high)


def front(image, part, parts, own, sources, source_map, matrices, box_gain):
    _, points, boxes = sources.shape
    ranks = source_map.shape[0]
    cols = boxes // 2 // parts
    grid_spec = pltpu.PrefetchScalarGridSpec(
        num_scalar_prefetch=1,
        grid=(1,),
        in_specs=[
            pl.BlockSpec((1, points, cols), lambda i, s: (image, 0, part)),
            pl.BlockSpec((1, points, cols), lambda i, s: (image, 0, parts + part)),
            pl.BlockSpec((ranks, points), lambda i, s: (0, 0)),
            pl.BlockSpec((LOCAL_LEVELS,) + matrices.shape[1:], lambda i, s: (0, 0, 0)),
            pl.BlockSpec((LOCAL_LEVELS, cols), lambda i, s: (0, part)),
            pl.BlockSpec((LOCAL_LEVELS, cols), lambda i, s: (0, parts + part)),
        ],
        out_specs=[pl.BlockSpec((ranks, cols), lambda i, s: (0, 0))] * 2,
    )
    return pl.pallas_call(
        functools.partial(front_kernel, LOCAL_LEVELS),
        grid_spec=grid_spec,
        out_shape=[jax.ShapeDtypeStruct((ranks, cols), BF16)] * 2,
        compiler_params=params(FRONT_LIMIT),
        cost_estimate=cost(2 * cols * ranks * (points + LOCAL_LEVELS * 2 * ranks) * 8, 2 * cols * points * 2),
        name="source_map_and_local_levels",
    )(own, sources, sources, source_map, matrices, box_gain, box_gain)


def swap_kernel(level, own_ref, kept_in, recv_in, tr_ref, gl_ref, gh_ref, kept_ref, sent_ref):
    gains = gl_ref[level : level + 1, :], gh_ref[level : level + 1, :]
    low, high = pick(own_ref[0], kept_in[...], recv_in[...])
    low, high = pair(tr_ref[level], low, high, gains)
    kept_ref[...], sent_ref[...] = pick(own_ref[1], low, high)


def upper_level(level, part, parts, owns, kept, received, matrices, box_gain):
    ranks, cols = kept.shape
    block = pl.BlockSpec((ranks, cols), lambda i, s: (0, 0))
    grid_spec = pltpu.PrefetchScalarGridSpec(
        num_scalar_prefetch=1,
        grid=(1,),
        in_specs=[
            block,
            block,
            pl.BlockSpec(matrices.shape, lambda i, s: (0, 0, 0)),
            pl.BlockSpec((box_gain.shape[0], cols), lambda i, s: (0, part)),
            pl.BlockSpec((box_gain.shape[0], cols), lambda i, s: (0, parts + part)),
        ],
        out_specs=[block] * 2,
    )
    return pl.pallas_call(
        functools.partial(swap_kernel, level),
        grid_spec=grid_spec,
        out_shape=[jax.ShapeDtypeStruct(kept.shape, BF16)] * 2,
        compiler_params=params(),
        cost_estimate=cost(cols * 4 * ranks * ranks * 8, cols * ranks * 8),
        name="upper_level",
    )(owns, kept, received, matrices, box_gain, box_gain)


def rows_kernel(level, images, own_ref, *refs):
    parts, (tr_ref, gl_ref, gh_ref), out_ref = refs[: 2 * images], refs[2 * images : 2 * images + 3], refs[-1]
    gains = gl_ref[level : level + 1, :], gh_ref[level : level + 1, :]
    lows, highs = [], []
    for c in range(images):
        low, high = pick(own_ref[0], parts[c][...], parts[images + c][...])
        low, high = pair(tr_ref[level], low, high, gains)
        lows.append(low)
        highs.append(high)
    piece = gl_ref.shape[1] // out_ref.shape[1]
    width = out_ref.shape[3]
    later = [ref[i : i + 1, :] for i in range(level + 1, gl_ref.shape[0] - 1) for ref in (gl_ref, gh_ref)]
    blank = jnp.zeros((1, width), F32)
    for k in range(out_ref.shape[1]):
        rows = [row[:, at : at + width] for at in range(k * piece, (k + 1) * piece, width) for row in later]
        rows += [blank] * (out_ref.shape[2] - piece - len(rows))
        rows = jnp.concatenate(rows, axis=0).astype(BF16)
        for n in range(2):
            out_ref[n, k, piece:, :] = rows
    for n, blocks in enumerate((lows, highs)):
        stacked = jnp.concatenate(blocks, axis=0).astype(F32)
        for k in range(out_ref.shape[1]):
            out_ref[n, k, :piece, :] = stacked[:, k * piece : (k + 1) * piece].T.astype(BF16)


def rows_level(level, part, parts, owns, kept, received, matrices, box_gain, pieces, extra, before):
    images = len(kept)
    ranks, cols = kept[0].shape
    piece = 2 * parts * cols // pieces
    block = pl.BlockSpec((ranks, cols), lambda i, s: (0, 0))
    more = [] if before is None else [before]
    grid_spec = pltpu.PrefetchScalarGridSpec(
        num_scalar_prefetch=1,
        grid=(1,),
        in_specs=[block] * (2 * images)
        + [
            pl.BlockSpec(matrices.shape, lambda i, s: (0, 0, 0)),
            pl.BlockSpec((box_gain.shape[0], cols), lambda i, s: (0, part)),
            pl.BlockSpec((box_gain.shape[0], cols), lambda i, s: (0, parts + part)),
        ]
        + [pl.BlockSpec(memory_space=pl.ANY)] * len(more),
        out_specs=pl.BlockSpec(
            (2, cols // piece, piece + extra, images * ranks), lambda i, s: (0, part, 0, 0)
        ),
    )
    return pl.pallas_call(
        functools.partial(rows_kernel, level, images),
        grid_spec=grid_spec,
        out_shape=jax.ShapeDtypeStruct((2, pieces // 2, piece + extra, images * ranks), BF16),
        input_output_aliases={2 * images + 4: 0} if more else {},
        compiler_params=params(),
        cost_estimate=cost(images * cols * 4 * ranks * ranks * 8, images * cols * ranks * 8),
        name="upper_level_to_rows",
    )(owns, *kept, *received, matrices, box_gain, box_gain, *more)


UNROLL = 128


def gather_kernel(order_ref, rows_ref, out_ref, table, picked):
    boxes = table.shape[0]
    pieces = rows_ref.shape[0]
    chunk = boxes // pieces

    def widen(i, carry):
        table[pl.ds(pl.multiple_of(i * chunk, chunk), chunk), :] = rows_ref[i, :chunk, :].astype(F32)
        return carry

    lax.fori_loop(0, pieces, widen, 0)

    def move(i, carry):
        base = pl.multiple_of(i * UNROLL, UNROLL)
        for k in range(UNROLL):
            picked[pl.ds(base + k, 1), :] = table[pl.ds(order_ref[0, base + k], 1), :]
        return carry

    lax.fori_loop(0, boxes // UNROLL, move, 0)

    def narrow(i, carry):
        at = pl.ds(pl.multiple_of(i * chunk, chunk), chunk)
        out_ref[at, :] = picked[at, :].astype(BF16)
        return carry

    lax.fori_loop(0, boxes // chunk, narrow, 0)


def gather_rows(order, rows):
    boxes, width = order.shape[1], rows.shape[2]
    return pl.pallas_call(
        gather_kernel,
        in_specs=[
            pl.BlockSpec(memory_space=pltpu.SMEM),
            pl.BlockSpec(memory_space=pltpu.VMEM),
        ],
        out_specs=pl.BlockSpec(memory_space=pltpu.VMEM),
        out_shape=jax.ShapeDtypeStruct((boxes, width), BF16),
        scratch_shapes=[pltpu.VMEM((boxes, width), F32), pltpu.VMEM((boxes, width), F32)],
        compiler_params=params(),
        cost_estimate=cost(0, 30 * 2**20),
        name="box_order",
    )(order, rows)


def lower_kernel(levels, first, own_ref, x_ref, tr_ref, gain_ref, out_ref, held, scales):
    devices, cols, width = x_ref.shape
    images, ranks = out_ref.shape[1], out_ref.shape[2]
    half_at = own_ref[0] * (devices // 2)
    for g in range(devices // 2):
        scales[g] = gain_ref[half_at + g, cols:, :].astype(F32)
    for i in range(levels):
        bit = levels - 1 - i
        matrix = tr_ref[first + i]
        if i == 0:
            blank = jnp.zeros((2 * ranks, ranks), BF16)
            sides = []
            for side in range(2):
                part = matrix[:, side * ranks : (side + 1) * ranks]
                bands = [
                    jnp.concatenate([part if c == b else blank for b in range(images)], axis=1)
                    for c in range(images)
                ]
                sides.append(jnp.concatenate(bands, axis=0))
            both = jnp.concatenate(sides, axis=1)
        target = out_ref if i == levels - 1 else held
        for g in range(devices // 2):
            low_at = ((g >> bit) << (bit + 1)) | (g & ((1 << bit) - 1))
            high_at = low_at + (1 << bit)
            if i < levels - 1:
                gains = []
                for n in range(2):
                    at = [2 * (levels - 1) * k + 2 * i + n for k in range(cols // width)]
                    gains.append(jnp.concatenate([scales[g, r : r + 1, :] for r in at], axis=1))
            if i == 0:
                stacked = jnp.concatenate([x_ref[low_at], x_ref[high_at]], axis=1)
                product = lax.dot_general(
                    both, stacked, (((1,), (1,)), ((), ())), preferred_element_type=F32
                )
            for c in range(images):
                if i == 0:
                    own = product[c * 2 * ranks : (c + 1) * 2 * ranks]
                else:
                    own = dot(matrix, jnp.concatenate([held[low_at, c], held[high_at, c]], axis=0))
                low, high = own[:ranks], own[ranks:]
                if i < levels - 1:
                    low, high = low * gains[0], high * gains[1]
                target[low_at, c] = low.astype(BF16)
                target[high_at, c] = high.astype(BF16)


def lower_levels(own, x, matrices, gains, images, first):
    devices, cols, width = x.shape
    ranks = width // images
    levels = devices.bit_length() - 1
    shape = (devices, images, ranks, cols)
    return pl.pallas_call(
        functools.partial(lower_kernel, levels, first),
        in_specs=[pl.BlockSpec(memory_space=pltpu.SMEM)] + [pl.BlockSpec(memory_space=pltpu.VMEM)] * 3,
        out_specs=pl.BlockSpec(memory_space=pltpu.VMEM),
        out_shape=jax.ShapeDtypeStruct(shape, BF16),
        scratch_shapes=[
            pltpu.VMEM(shape, BF16),
            pltpu.VMEM((devices // 2, gains.shape[1] - cols, width), F32),
        ],
        compiler_params=params(),
        cost_estimate=cost(levels * devices * cols * 2 * width * ranks * 8, devices * width * cols * 4),
        name="lower_levels",
    )(own, x, matrices, gains)


def target_kernel(level, x_ref, map_ref, gain_ref, out_ref):
    pieces, _, images, ranks, cols = x_ref.shape
    target_map = map_ref[...].astype(F32).T.astype(BF16)
    for k in range(pieces):
        at = slice(k * cols, (k + 1) * cols)
        gains = gain_ref[level : level + 1, at]
        for c in range(images):
            scaled = (x_ref[k, 0, c].astype(F32) * gains).astype(BF16)
            out_ref[c, :, at] = dot(target_map, scaled).astype(BF16)


def to_targets(x, target_map, box_gain, pieces):
    t_pieces, two, images, ranks, cols = x.shape
    points = target_map.shape[1]
    per_half = t_pieces // pieces
    return pl.pallas_call(
        functools.partial(target_kernel, box_gain.shape[0] - 1),
        grid=(two, per_half),
        in_specs=[
            pl.BlockSpec((pieces, 1, images, ranks, cols), lambda n, i: (i, n, 0, 0, 0)),
            pl.BlockSpec((ranks, points), lambda n, i: (0, 0)),
            pl.BlockSpec((box_gain.shape[0], pieces * cols), lambda n, i: (0, n * per_half + i)),
        ],
        out_specs=pl.BlockSpec((images, points, pieces * cols), lambda n, i: (0, 0, n * per_half + i)),
        out_shape=jax.ShapeDtypeStruct((images, points, two * t_pieces * cols), BF16),
        compiler_params=params(),
        cost_estimate=cost(images * points * ranks * two * t_pieces * cols * 4, images * points * two * t_pieces * cols * 2),
        name="target_map",
    )(x, target_map, box_gain)


def body(sources, source_map, translation, box_gain, target_order, target_map):
    images, _, boxes = sources.shape
    ranks = source_map.shape[0]
    n_lower = lax.axis_size("lo")
    matrices = translation.reshape(translation.shape[0], 2 * ranks, 2 * ranks)
    upper = lax.axis_index("hi")
    owns = jnp.stack([upper >> 1 & 1, upper & 1]).astype(jnp.int32)
    first_lower = LOCAL_LEVELS + 2
    levels_lo = n_lower.bit_length() - 1
    piece = boxes // n_lower
    halves = n_lower // 2
    groups = [list(range(halves)), list(range(halves, n_lower))]

    own_half = (lax.axis_index("lo") >> levels_lo - 1).astype(jnp.int32).reshape(1)
    extra = -(-2 * (levels_lo - 1) * piece // (images * ranks) // 16) * 16

    kept, received = {}, {}
    for part in range(PARTS):
        for c in range(images):
            at = part, c
            kept[at], sent = front(c, part, PARTS, owns[:1], sources, source_map, matrices, box_gain)
            received[at] = lax.ppermute(sent, "hi", [(i, i ^ 2) for i in range(4)])
    rows, turn = None, own_half
    for part in range(PARTS):
        for c in range(images):
            at = part, c
            kept[at], sent = upper_level(
                LOCAL_LEVELS, part, PARTS, owns, kept[at], received[at], matrices, box_gain
            )
            turn, sent = lax.optimization_barrier((turn, sent))
            received[at] = lax.ppermute(sent, "hi", [(i, i ^ 1) for i in range(4)])
        rows = rows_level(
            LOCAL_LEVELS + 1,
            part,
            PARTS,
            owns[1:],
            [kept[part, c] for c in range(images)],
            [received[part, c] for c in range(images)],
            matrices,
            box_gain,
            n_lower,
            extra,
            rows,
        )
    for partner in PARTNERS:
        pairs = [(d, d ^ partner) for d in range(4 * n_lower) if d & n_lower]
        turn = lax.ppermute(turn, ("hi", "lo"), pairs)
    own_half, rows = lax.optimization_barrier((jnp.maximum(own_half, turn), rows))
    moved = lax.all_to_all(rows.reshape(n_lower, piece + extra, images * ranks), "lo", 0, 0)
    rows = gather_rows(target_order, moved)
    rows = lax.all_to_all(rows.reshape(n_lower, piece, images * ranks), "lo", 0, 0)
    blocks = lower_levels(own_half, rows, matrices, moved, images, first_lower)
    blocks = blocks.reshape(halves, 2, images, ranks, piece)
    blocks = lax.all_to_all(blocks, "lo", 0, 0, axis_index_groups=groups)
    return to_targets(blocks, target_map.T, box_gain, 8)


def solution(mesh):
    return jax.shard_map(
        body,
        mesh=mesh,
        in_specs=(
            P(None, None, ("hi", "lo")),
            P(),
            P(),
            P(None, ("hi", "lo")),
            P(("hi", "lo"), None),
            P(),
        ),
        out_specs=P(None, None, ("hi", "lo")),
        check_vma=False,
    )
```

```python
import functools

import jax
import jax.numpy as jnp
from jax import lax
from jax.experimental import pallas as pl
from jax.experimental.pallas import tpu as pltpu
from jax.sharding import PartitionSpec as P

LOCAL_LEVELS = 8
F32 = jnp.float32
BF16 = jnp.bfloat16
VMEM_LIMIT = 40 * 2**20
FRONT_LIMIT = 56 * 2**20
PARTS = 1
PARTNERS = 74, 66


def dot(a, b):
    return jnp.dot(a, b, preferred_element_type=F32)


def params(limit=VMEM_LIMIT):
    return pltpu.CompilerParams(vmem_limit_bytes=limit)


def cost(macs, moved):
    return pl.CostEstimate(flops=2 * macs, bytes_accessed=moved, transcendentals=0)


def pick(own, kept, received):
    first = own == 0
    return jnp.where(first, kept, received), jnp.where(first, received, kept)


def pair(matrix, low, high, gains):
    ranks = low.shape[0]
    product = dot(matrix, jnp.concatenate([low, high], axis=0))
    return (
        (product[:ranks] * gains[0]).astype(BF16),
        (product[ranks:] * gains[1]).astype(BF16),
    )


def front_kernel(levels, own_ref, low_ref, high_ref, map_ref, tr_ref, gl_ref, gh_ref, kept_ref, sent_ref):
    source_map = map_ref[...]
    low = dot(source_map, low_ref[0]).astype(BF16)
    high = dot(source_map, high_ref[0]).astype(BF16)
    for level in range(levels):
        gains = gl_ref[level : level + 1, :], gh_ref[level : level + 1, :]
        low, high = pair(tr_ref[level], low, high, gains)
    kept_ref[...], sent_ref[...] = pick(own_ref[0], low, high)


def front(image, part, parts, own, sources, source_map, matrices, box_gain):
    _, points, boxes = sources.shape
    ranks = source_map.shape[0]
    cols = boxes // 2 // parts
    grid_spec = pltpu.PrefetchScalarGridSpec(
        num_scalar_prefetch=1,
        grid=(1,),
        in_specs=[
            pl.BlockSpec((1, points, cols), lambda i, s: (image, 0, part)),
            pl.BlockSpec((1, points, cols), lambda i, s: (image, 0, parts + part)),
            pl.BlockSpec((ranks, points), lambda i, s: (0, 0)),
            pl.BlockSpec((LOCAL_LEVELS,) + matrices.shape[1:], lambda i, s: (0, 0, 0)),
            pl.BlockSpec((LOCAL_LEVELS, cols), lambda i, s: (0, part)),
            pl.BlockSpec((LOCAL_LEVELS, cols), lambda i, s: (0, parts + part)),
        ],
        out_specs=[pl.BlockSpec((ranks, cols), lambda i, s: (0, 0))] * 2,
    )
    return pl.pallas_call(
        functools.partial(front_kernel, LOCAL_LEVELS),
        grid_spec=grid_spec,
        out_shape=[jax.ShapeDtypeStruct((ranks, cols), BF16)] * 2,
        compiler_params=params(FRONT_LIMIT),
        cost_estimate=cost(2 * cols * ranks * (points + LOCAL_LEVELS * 2 * ranks) * 8, 2 * cols * points * 2),
        name="source_map_and_local_levels",
    )(own, sources, sources, source_map, matrices, box_gain, box_gain)


def swap_kernel(level, own_ref, kept_in, recv_in, tr_ref, gl_ref, gh_ref, kept_ref, sent_ref):
    gains = gl_ref[level : level + 1, :], gh_ref[level : level + 1, :]
    low, high = pick(own_ref[0], kept_in[...], recv_in[...])
    low, high = pair(tr_ref[level], low, high, gains)
    kept_ref[...], sent_ref[...] = pick(own_ref[1], low, high)


def upper_level(level, part, parts, owns, kept, received, matrices, box_gain):
    ranks, cols = kept.shape
    block = pl.BlockSpec((ranks, cols), lambda i, s: (0, 0))
    grid_spec = pltpu.PrefetchScalarGridSpec(
        num_scalar_prefetch=1,
        grid=(1,),
        in_specs=[
            block,
            block,
            pl.BlockSpec(matrices.shape, lambda i, s: (0, 0, 0)),
            pl.BlockSpec((box_gain.shape[0], cols), lambda i, s: (0, part)),
            pl.BlockSpec((box_gain.shape[0], cols), lambda i, s: (0, parts + part)),
        ],
        out_specs=[block] * 2,
    )
    return pl.pallas_call(
        functools.partial(swap_kernel, level),
        grid_spec=grid_spec,
        out_shape=[jax.ShapeDtypeStruct(kept.shape, BF16)] * 2,
        compiler_params=params(),
        cost_estimate=cost(cols * 4 * ranks * ranks * 8, cols * ranks * 8),
        name="upper_level",
    )(owns, kept, received, matrices, box_gain, box_gain)


def rows_kernel(level, images, own_ref, *refs):
    parts, (tr_ref, gl_ref, gh_ref), out_ref = refs[: 2 * images], refs[2 * images : 2 * images + 3], refs[-1]
    gains = gl_ref[level : level + 1, :], gh_ref[level : level + 1, :]
    lows, highs = [], []
    for c in range(images):
        low, high = pick(own_ref[0], parts[c][...], parts[images + c][...])
        low, high = pair(tr_ref[level], low, high, gains)
        lows.append(low)
        highs.append(high)
    piece = gl_ref.shape[1] // out_ref.shape[1]
    width = out_ref.shape[3]
    later = [ref[i : i + 1, :] for i in range(level + 1, gl_ref.shape[0] - 1) for ref in (gl_ref, gh_ref)]
    blank = jnp.zeros((1, width), F32)
    for k in range(out_ref.shape[1]):
        rows = [row[:, at : at + width] for at in range(k * piece, (k + 1) * piece, width) for row in later]
        rows += [blank] * (out_ref.shape[2] - piece - len(rows))
        rows = jnp.concatenate(rows, axis=0).astype(BF16)
        for n in range(2):
            out_ref[n, k, piece:, :] = rows
    for n, blocks in enumerate((lows, highs)):
        stacked = jnp.concatenate(blocks, axis=0).astype(F32)
        for k in range(out_ref.shape[1]):
            out_ref[n, k, :piece, :] = stacked[:, k * piece : (k + 1) * piece].T.astype(BF16)


def rows_level(level, part, parts, owns, kept, received, matrices, box_gain, pieces, extra, before):
    images = len(kept)
    ranks, cols = kept[0].shape
    piece = 2 * parts * cols // pieces
    block = pl.BlockSpec((ranks, cols), lambda i, s: (0, 0))
    more = [] if before is None else [before]
    grid_spec = pltpu.PrefetchScalarGridSpec(
        num_scalar_prefetch=1,
        grid=(1,),
        in_specs=[block] * (2 * images)
        + [
            pl.BlockSpec(matrices.shape, lambda i, s: (0, 0, 0)),
            pl.BlockSpec((box_gain.shape[0], cols), lambda i, s: (0, part)),
            pl.BlockSpec((box_gain.shape[0], cols), lambda i, s: (0, parts + part)),
        ]
        + [pl.BlockSpec(memory_space=pl.ANY)] * len(more),
        out_specs=pl.BlockSpec(
            (2, cols // piece, piece + extra, images * ranks), lambda i, s: (0, part, 0, 0)
        ),
    )
    return pl.pallas_call(
        functools.partial(rows_kernel, level, images),
        grid_spec=grid_spec,
        out_shape=jax.ShapeDtypeStruct((2, pieces // 2, piece + extra, images * ranks), BF16),
        input_output_aliases={2 * images + 4: 0} if more else {},
        compiler_params=params(),
        cost_estimate=cost(images * cols * 4 * ranks * ranks * 8, images * cols * ranks * 8),
        name="upper_level_to_rows",
    )(owns, *kept, *received, matrices, box_gain, box_gain, *more)


UNROLL = 512


def gather_kernel(order_ref, rows_ref, out_ref, table, picked):
    boxes = table.shape[0]
    pieces = rows_ref.shape[0]
    chunk = boxes // pieces

    def widen(i, carry):
        table[pl.ds(pl.multiple_of(i * chunk, chunk), chunk), :] = rows_ref[i, :chunk, :].astype(F32)
        return carry

    lax.fori_loop(0, pieces, widen, 0)

    def move(i, carry):
        base = pl.multiple_of(i * UNROLL, UNROLL)
        for k in range(UNROLL):
            picked[k : k + 1, :] = table[pl.ds(order_ref[0, base + k], 1), :]
        out_ref[pl.ds(base, UNROLL), :] = picked[...].astype(BF16)
        return carry

    lax.fori_loop(0, boxes // UNROLL, move, 0)


def gather_rows(order, rows):
    boxes, width = order.shape[1], rows.shape[2]
    return pl.pallas_call(
        gather_kernel,
        in_specs=[
            pl.BlockSpec(memory_space=pltpu.SMEM),
            pl.BlockSpec(memory_space=pltpu.VMEM),
        ],
        out_specs=pl.BlockSpec(memory_space=pltpu.VMEM),
        out_shape=jax.ShapeDtypeStruct((boxes, width), BF16),
        scratch_shapes=[pltpu.VMEM((boxes, width), F32), pltpu.VMEM((UNROLL, width), F32)],
        compiler_params=params(),
        cost_estimate=cost(0, 30 * 2**20),
        name="box_order",
    )(order, rows)


def lower_kernel(levels, first, own_ref, x_ref, tr_ref, gain_ref, out_ref, held, scales):
    devices, cols, width = x_ref.shape
    images, ranks = out_ref.shape[1], out_ref.shape[2]
    half_at = own_ref[0] * (devices // 2)
    for g in range(devices // 2):
        scales[g] = gain_ref[half_at + g, cols:, :].astype(F32)
    for i in range(levels):
        bit = levels - 1 - i
        matrix = tr_ref[first + i]
        if i == 0:
            blank = jnp.zeros((2 * ranks, ranks), BF16)
            sides = []
            for side in range(2):
                part = matrix[:, side * ranks : (side + 1) * ranks]
                bands = [
                    jnp.concatenate([part if c == b else blank for b in range(images)], axis=1)
                    for c in range(images)
                ]
                sides.append(jnp.concatenate(bands, axis=0))
            both = jnp.concatenate(sides, axis=1)
        target = out_ref if i == levels - 1 else held
        for g in range(devices // 2):
            low_at = ((g >> bit) << (bit + 1)) | (g & ((1 << bit) - 1))
            high_at = low_at + (1 << bit)
            if i < levels - 1:
                gains = []
                for n in range(2):
                    at = [2 * (levels - 1) * k + 2 * i + n for k in range(cols // width)]
                    gains.append(jnp.concatenate([scales[g, r : r + 1, :] for r in at], axis=1))
            if i == 0:
                stacked = jnp.concatenate([x_ref[low_at], x_ref[high_at]], axis=1)
                product = lax.dot_general(
                    both, stacked, (((1,), (1,)), ((), ())), preferred_element_type=F32
                )
            for c in range(images):
                if i == 0:
                    own = product[c * 2 * ranks : (c + 1) * 2 * ranks]
                else:
                    own = dot(matrix, jnp.concatenate([held[low_at, c], held[high_at, c]], axis=0))
                low, high = own[:ranks], own[ranks:]
                if i < levels - 1:
                    low, high = low * gains[0], high * gains[1]
                target[low_at, c] = low.astype(BF16)
                target[high_at, c] = high.astype(BF16)


def lower_levels(own, x, matrices, gains, images, first):
    devices, cols, width = x.shape
    ranks = width // images
    levels = devices.bit_length() - 1
    shape = (devices, images, ranks, cols)
    return pl.pallas_call(
        functools.partial(lower_kernel, levels, first),
        in_specs=[pl.BlockSpec(memory_space=pltpu.SMEM)] + [pl.BlockSpec(memory_space=pltpu.VMEM)] * 3,
        out_specs=pl.BlockSpec(memory_space=pltpu.VMEM),
        out_shape=jax.ShapeDtypeStruct(shape, BF16),
        scratch_shapes=[
            pltpu.VMEM(shape, BF16),
            pltpu.VMEM((devices // 2, gains.shape[1] - cols, width), F32),
        ],
        compiler_params=params(),
        cost_estimate=cost(levels * devices * cols * 2 * width * ranks * 8, devices * width * cols * 4),
        name="lower_levels",
    )(own, x, matrices, gains)


def target_kernel(level, x_ref, map_ref, gain_ref, out_ref):
    pieces, _, images, ranks, cols = x_ref.shape
    target_map = map_ref[...].astype(F32).T.astype(BF16)
    for k in range(pieces):
        at = slice(k * cols, (k + 1) * cols)
        gains = gain_ref[level : level + 1, at]
        for c in range(images):
            scaled = (x_ref[k, 0, c].astype(F32) * gains).astype(BF16)
            out_ref[c, :, at] = dot(target_map, scaled).astype(BF16)


def to_targets(x, target_map, box_gain, pieces):
    t_pieces, two, images, ranks, cols = x.shape
    points = target_map.shape[1]
    per_half = t_pieces // pieces
    return pl.pallas_call(
        functools.partial(target_kernel, box_gain.shape[0] - 1),
        grid=(two, per_half),
        in_specs=[
            pl.BlockSpec((pieces, 1, images, ranks, cols), lambda n, i: (i, n, 0, 0, 0)),
            pl.BlockSpec((ranks, points), lambda n, i: (0, 0)),
            pl.BlockSpec((box_gain.shape[0], pieces * cols), lambda n, i: (0, n * per_half + i)),
        ],
        out_specs=pl.BlockSpec((images, points, pieces * cols), lambda n, i: (0, 0, n * per_half + i)),
        out_shape=jax.ShapeDtypeStruct((images, points, two * t_pieces * cols), BF16),
        compiler_params=params(),
        cost_estimate=cost(images * points * ranks * two * t_pieces * cols * 4, images * points * two * t_pieces * cols * 2),
        name="target_map",
    )(x, target_map, box_gain)


def body(sources, source_map, translation, box_gain, target_order, target_map):
    images, _, boxes = sources.shape
    ranks = source_map.shape[0]
    n_lower = lax.axis_size("lo")
    matrices = translation.reshape(translation.shape[0], 2 * ranks, 2 * ranks)
    upper = lax.axis_index("hi")
    owns = jnp.stack([upper >> 1 & 1, upper & 1]).astype(jnp.int32)
    first_lower = LOCAL_LEVELS + 2
    levels_lo = n_lower.bit_length() - 1
    piece = boxes // n_lower
    halves = n_lower // 2
    groups = [list(range(halves)), list(range(halves, n_lower))]

    own_half = (lax.axis_index("lo") >> levels_lo - 1).astype(jnp.int32).reshape(1)
    extra = -(-2 * (levels_lo - 1) * piece // (images * ranks) // 16) * 16

    kept, received = {}, {}
    for part in range(PARTS):
        for c in range(images):
            at = part, c
            kept[at], sent = front(c, part, PARTS, owns[:1], sources, source_map, matrices, box_gain)
            received[at] = lax.ppermute(sent, "hi", [(i, i ^ 2) for i in range(4)])
    rows, turn = None, own_half
    for part in range(PARTS):
        for c in range(images):
            at = part, c
            kept[at], sent = upper_level(
                LOCAL_LEVELS, part, PARTS, owns, kept[at], received[at], matrices, box_gain
            )
            turn, sent = lax.optimization_barrier((turn, sent))
            received[at] = lax.ppermute(sent, "hi", [(i, i ^ 1) for i in range(4)])
        rows = rows_level(
            LOCAL_LEVELS + 1,
            part,
            PARTS,
            owns[1:],
            [kept[part, c] for c in range(images)],
            [received[part, c] for c in range(images)],
            matrices,
            box_gain,
            n_lower,
            extra,
            rows,
        )
    for partner in PARTNERS:
        pairs = [(d, d ^ partner) for d in range(4 * n_lower) if d & n_lower]
        turn = lax.ppermute(turn, ("hi", "lo"), pairs)
    own_half, rows = lax.optimization_barrier((jnp.maximum(own_half, turn), rows))
    moved = lax.all_to_all(rows.reshape(n_lower, piece + extra, images * ranks), "lo", 0, 0)
    rows = gather_rows(target_order, moved)
    rows = lax.all_to_all(rows.reshape(n_lower, piece, images * ranks), "lo", 0, 0)
    blocks = lower_levels(own_half, rows, matrices, moved, images, first_lower)
    blocks = blocks.reshape(halves, 2, images, ranks, piece)
    blocks = lax.all_to_all(blocks, "lo", 0, 0, axis_index_groups=groups)
    return to_targets(blocks, target_map.T, box_gain, 16)


def solution(mesh):
    return jax.shard_map(
        body,
        mesh=mesh,
        in_specs=(
            P(None, None, ("hi", "lo")),
            P(),
            P(),
            P(None, ("hi", "lo")),
            P(("hi", "lo"), None),
            P(),
        ),
        out_specs=P(None, None, ("hi", "lo")),
        check_vma=False,
    )
```

```python
import functools

import jax
import jax.numpy as jnp
from jax import lax
from jax.experimental import pallas as pl
from jax.experimental.pallas import tpu as pltpu
from jax.sharding import PartitionSpec as P

LOCAL_LEVELS = 8
F32 = jnp.float32
BF16 = jnp.bfloat16
VMEM_LIMIT = 40 * 2**20
FRONT_LIMIT = 56 * 2**20
PARTS = 1
PARTNERS = 74, 66


def dot(a, b):
    return jnp.dot(a, b, preferred_element_type=F32)


def params(limit=VMEM_LIMIT):
    return pltpu.CompilerParams(vmem_limit_bytes=limit)


def cost(macs, moved):
    return pl.CostEstimate(flops=2 * macs, bytes_accessed=moved, transcendentals=0)


def pick(own, kept, received):
    first = own == 0
    return jnp.where(first, kept, received), jnp.where(first, received, kept)


def pair(matrix, low, high, gains):
    ranks = low.shape[0]
    product = dot(matrix, jnp.concatenate([low, high], axis=0))
    return (
        (product[:ranks] * gains[0]).astype(BF16),
        (product[ranks:] * gains[1]).astype(BF16),
    )


def front_kernel(levels, own_ref, low_ref, high_ref, map_ref, tr_ref, gl_ref, gh_ref, kept_ref, sent_ref):
    source_map = map_ref[...]
    low = dot(source_map, low_ref[0]).astype(BF16)
    high = dot(source_map, high_ref[0]).astype(BF16)
    for level in range(levels):
        gains = gl_ref[level : level + 1, :], gh_ref[level : level + 1, :]
        low, high = pair(tr_ref[level], low, high, gains)
    kept_ref[...], sent_ref[...] = pick(own_ref[0], low, high)


def front(image, part, parts, own, sources, source_map, matrices, box_gain):
    _, points, boxes = sources.shape
    ranks = source_map.shape[0]
    cols = boxes // 2 // parts
    grid_spec = pltpu.PrefetchScalarGridSpec(
        num_scalar_prefetch=1,
        grid=(1,),
        in_specs=[
            pl.BlockSpec((1, points, cols), lambda i, s: (image, 0, part)),
            pl.BlockSpec((1, points, cols), lambda i, s: (image, 0, parts + part)),
            pl.BlockSpec((ranks, points), lambda i, s: (0, 0)),
            pl.BlockSpec((LOCAL_LEVELS,) + matrices.shape[1:], lambda i, s: (0, 0, 0)),
            pl.BlockSpec((LOCAL_LEVELS, cols), lambda i, s: (0, part)),
            pl.BlockSpec((LOCAL_LEVELS, cols), lambda i, s: (0, parts + part)),
        ],
        out_specs=[pl.BlockSpec((ranks, cols), lambda i, s: (0, 0))] * 2,
    )
    return pl.pallas_call(
        functools.partial(front_kernel, LOCAL_LEVELS),
        grid_spec=grid_spec,
        out_shape=[jax.ShapeDtypeStruct((ranks, cols), BF16)] * 2,
        compiler_params=params(FRONT_LIMIT),
        cost_estimate=cost(2 * cols * ranks * (points + LOCAL_LEVELS * 2 * ranks) * 8, 2 * cols * points * 2),
        name="source_map_and_local_levels",
    )(own, sources, sources, source_map, matrices, box_gain, box_gain)


def swap_kernel(level, own_ref, kept_in, recv_in, tr_ref, gl_ref, gh_ref, kept_ref, sent_ref):
    gains = gl_ref[level : level + 1, :], gh_ref[level : level + 1, :]
    low, high = pick(own_ref[0], kept_in[...], recv_in[...])
    low, high = pair(tr_ref[level], low, high, gains)
    kept_ref[...], sent_ref[...] = pick(own_ref[1], low, high)


def upper_level(level, part, parts, owns, kept, received, matrices, box_gain):
    ranks, cols = kept.shape
    block = pl.BlockSpec((ranks, cols), lambda i, s: (0, 0))
    grid_spec = pltpu.PrefetchScalarGridSpec(
        num_scalar_prefetch=1,
        grid=(1,),
        in_specs=[
            block,
            block,
            pl.BlockSpec(matrices.shape, lambda i, s: (0, 0, 0)),
            pl.BlockSpec((box_gain.shape[0], cols), lambda i, s: (0, part)),
            pl.BlockSpec((box_gain.shape[0], cols), lambda i, s: (0, parts + part)),
        ],
        out_specs=[block] * 2,
    )
    return pl.pallas_call(
        functools.partial(swap_kernel, level),
        grid_spec=grid_spec,
        out_shape=[jax.ShapeDtypeStruct(kept.shape, BF16)] * 2,
        compiler_params=params(),
        cost_estimate=cost(cols * 4 * ranks * ranks * 8, cols * ranks * 8),
        name="upper_level",
    )(owns, kept, received, matrices, box_gain, box_gain)


def rows_kernel(level, images, own_ref, *refs):
    parts, (tr_ref, gl_ref, gh_ref), out_ref = refs[: 2 * images], refs[2 * images : 2 * images + 3], refs[-1]
    gains = gl_ref[level : level + 1, :], gh_ref[level : level + 1, :]
    lows, highs = [], []
    for c in range(images):
        low, high = pick(own_ref[0], parts[c][...], parts[images + c][...])
        low, high = pair(tr_ref[level], low, high, gains)
        lows.append(low)
        highs.append(high)
    piece = gl_ref.shape[1] // out_ref.shape[1]
    width = out_ref.shape[3]
    later = [ref[i : i + 1, :] for i in range(level + 1, gl_ref.shape[0] - 1) for ref in (gl_ref, gh_ref)]
    blank = jnp.zeros((1, width), F32)
    for k in range(out_ref.shape[1]):
        rows = [row[:, at : at + width] for at in range(k * piece, (k + 1) * piece, width) for row in later]
        rows += [blank] * (out_ref.shape[2] - piece - len(rows))
        rows = jnp.concatenate(rows, axis=0).astype(BF16)
        for n in range(2):
            out_ref[n, k, piece:, :] = rows
    for n, blocks in enumerate((lows, highs)):
        stacked = jnp.concatenate(blocks, axis=0).astype(F32)
        for k in range(out_ref.shape[1]):
            out_ref[n, k, :piece, :] = stacked[:, k * piece : (k + 1) * piece].T.astype(BF16)


def rows_level(level, part, parts, owns, kept, received, matrices, box_gain, pieces, extra, before):
    images = len(kept)
    ranks, cols = kept[0].shape
    piece = 2 * parts * cols // pieces
    block = pl.BlockSpec((ranks, cols), lambda i, s: (0, 0))
    more = [] if before is None else [before]
    grid_spec = pltpu.PrefetchScalarGridSpec(
        num_scalar_prefetch=1,
        grid=(1,),
        in_specs=[block] * (2 * images)
        + [
            pl.BlockSpec(matrices.shape, lambda i, s: (0, 0, 0)),
            pl.BlockSpec((box_gain.shape[0], cols), lambda i, s: (0, part)),
            pl.BlockSpec((box_gain.shape[0], cols), lambda i, s: (0, parts + part)),
        ]
        + [pl.BlockSpec(memory_space=pl.ANY)] * len(more),
        out_specs=pl.BlockSpec(
            (2, cols // piece, piece + extra, images * ranks), lambda i, s: (0, part, 0, 0)
        ),
    )
    return pl.pallas_call(
        functools.partial(rows_kernel, level, images),
        grid_spec=grid_spec,
        out_shape=jax.ShapeDtypeStruct((2, pieces // 2, piece + extra, images * ranks), BF16),
        input_output_aliases={2 * images + 4: 0} if more else {},
        compiler_params=params(),
        cost_estimate=cost(images * cols * 4 * ranks * ranks * 8, images * cols * ranks * 8),
        name="upper_level_to_rows",
    )(owns, *kept, *received, matrices, box_gain, box_gain, *more)


UNROLL = 512


def gather_kernel(order_ref, rows_ref, out_ref, table, picked):
    boxes = table.shape[0]
    pieces = rows_ref.shape[0]
    chunk = boxes // pieces

    def widen(i, carry):
        table[pl.ds(pl.multiple_of(i * chunk, chunk), chunk), :] = rows_ref[i, :chunk, :].astype(F32)
        return carry

    lax.fori_loop(0, pieces, widen, 0, unroll=4)

    def move(i, carry):
        base = pl.multiple_of(i * UNROLL, UNROLL)
        for k in range(UNROLL):
            picked[k : k + 1, :] = table[pl.ds(order_ref[0, base + k], 1), :]
        out_ref[pl.ds(base, UNROLL), :] = picked[...].astype(BF16)
        return carry

    lax.fori_loop(0, boxes // UNROLL, move, 0)


def gather_rows(order, rows):
    boxes, width = order.shape[1], rows.shape[2]
    return pl.pallas_call(
        gather_kernel,
        in_specs=[
            pl.BlockSpec(memory_space=pltpu.SMEM),
            pl.BlockSpec(memory_space=pltpu.VMEM),
        ],
        out_specs=pl.BlockSpec(memory_space=pltpu.VMEM),
        out_shape=jax.ShapeDtypeStruct((boxes, width), BF16),
        scratch_shapes=[pltpu.VMEM((boxes, width), F32), pltpu.VMEM((UNROLL, width), F32)],
        compiler_params=params(),
        cost_estimate=cost(0, 30 * 2**20),
        name="box_order",
    )(order, rows)


def lower_kernel(levels, first, own_ref, x_ref, tr_ref, gain_ref, out_ref, held, scales):
    devices, cols, width = x_ref.shape
    images, ranks = out_ref.shape[1], out_ref.shape[2]
    half_at = own_ref[0] * (devices // 2)
    for g in range(devices // 2):
        scales[g] = gain_ref[half_at + g, cols:, :].astype(F32)
    for i in range(levels):
        bit = levels - 1 - i
        matrix = tr_ref[first + i]
        if i == 0:
            blank = jnp.zeros((2 * ranks, ranks), BF16)
            sides = []
            for side in range(2):
                part = matrix[:, side * ranks : (side + 1) * ranks]
                bands = [
                    jnp.concatenate([part if c == b else blank for b in range(images)], axis=1)
                    for c in range(images)
                ]
                sides.append(jnp.concatenate(bands, axis=0))
            both = jnp.concatenate(sides, axis=1)
        target = out_ref if i == levels - 1 else held
        for g in range(devices // 2):
            low_at = ((g >> bit) << (bit + 1)) | (g & ((1 << bit) - 1))
            high_at = low_at + (1 << bit)
            if i < levels - 1:
                gains = []
                for n in range(2):
                    at = [2 * (levels - 1) * k + 2 * i + n for k in range(cols // width)]
                    gains.append(jnp.concatenate([scales[g, r : r + 1, :] for r in at], axis=1))
            if i == 0:
                stacked = jnp.concatenate([x_ref[low_at], x_ref[high_at]], axis=1)
                product = lax.dot_general(
                    both, stacked, (((1,), (1,)), ((), ())), preferred_element_type=F32
                )
            for c in range(images):
                if i == 0:
                    own = product[c * 2 * ranks : (c + 1) * 2 * ranks]
                else:
                    own = dot(matrix, jnp.concatenate([held[low_at, c], held[high_at, c]], axis=0))
                low, high = own[:ranks], own[ranks:]
                if i < levels - 1:
                    low, high = low * gains[0], high * gains[1]
                target[low_at, c] = low.astype(BF16)
                target[high_at, c] = high.astype(BF16)


def lower_levels(own, x, matrices, gains, images, first):
    devices, cols, width = x.shape
    ranks = width // images
    levels = devices.bit_length() - 1
    shape = (devices, images, ranks, cols)
    return pl.pallas_call(
        functools.partial(lower_kernel, levels, first),
        in_specs=[pl.BlockSpec(memory_space=pltpu.SMEM)] + [pl.BlockSpec(memory_space=pltpu.VMEM)] * 3,
        out_specs=pl.BlockSpec(memory_space=pltpu.VMEM),
        out_shape=jax.ShapeDtypeStruct(shape, BF16),
        scratch_shapes=[
            pltpu.VMEM(shape, BF16),
            pltpu.VMEM((devices // 2, gains.shape[1] - cols, width), F32),
        ],
        compiler_params=params(),
        cost_estimate=cost(levels * devices * cols * 2 * width * ranks * 8, devices * width * cols * 4),
        name="lower_levels",
    )(own, x, matrices, gains)


def target_kernel(level, x_ref, map_ref, gain_ref, out_ref):
    pieces, _, images, ranks, cols = x_ref.shape
    target_map = map_ref[...].astype(F32).T.astype(BF16)
    for k in range(pieces):
        at = slice(k * cols, (k + 1) * cols)
        gains = gain_ref[level : level + 1, at]
        for c in range(images):
            scaled = (x_ref[k, 0, c].astype(F32) * gains).astype(BF16)
            out_ref[c, :, at] = dot(target_map, scaled).astype(BF16)


def to_targets(x, target_map, box_gain, pieces):
    t_pieces, two, images, ranks, cols = x.shape
    points = target_map.shape[1]
    per_half = t_pieces // pieces
    return pl.pallas_call(
        functools.partial(target_kernel, box_gain.shape[0] - 1),
        grid=(two, per_half),
        in_specs=[
            pl.BlockSpec((pieces, 1, images, ranks, cols), lambda n, i: (i, n, 0, 0, 0)),
            pl.BlockSpec((ranks, points), lambda n, i: (0, 0)),
            pl.BlockSpec((box_gain.shape[0], pieces * cols), lambda n, i: (0, n * per_half + i)),
        ],
        out_specs=pl.BlockSpec((images, points, pieces * cols), lambda n, i: (0, 0, n * per_half + i)),
        out_shape=jax.ShapeDtypeStruct((images, points, two * t_pieces * cols), BF16),
        compiler_params=params(),
        cost_estimate=cost(images * points * ranks * two * t_pieces * cols * 4, images * points * two * t_pieces * cols * 2),
        name="target_map",
    )(x, target_map, box_gain)


def body(sources, source_map, translation, box_gain, target_order, target_map):
    images, _, boxes = sources.shape
    ranks = source_map.shape[0]
    n_lower = lax.axis_size("lo")
    matrices = translation.reshape(translation.shape[0], 2 * ranks, 2 * ranks)
    upper = lax.axis_index("hi")
    owns = jnp.stack([upper >> 1 & 1, upper & 1]).astype(jnp.int32)
    first_lower = LOCAL_LEVELS + 2
    levels_lo = n_lower.bit_length() - 1
    piece = boxes // n_lower
    halves = n_lower // 2
    groups = [list(range(halves)), list(range(halves, n_lower))]

    own_half = (lax.axis_index("lo") >> levels_lo - 1).astype(jnp.int32).reshape(1)
    extra = -(-2 * (levels_lo - 1) * piece // (images * ranks) // 16) * 16

    kept, received = {}, {}
    for part in range(PARTS):
        for c in range(images):
            at = part, c
            kept[at], sent = front(c, part, PARTS, owns[:1], sources, source_map, matrices, box_gain)
            received[at] = lax.ppermute(sent, "hi", [(i, i ^ 2) for i in range(4)])
    rows, turn = None, own_half
    for part in range(PARTS):
        for c in range(images):
            at = part, c
            kept[at], sent = upper_level(
                LOCAL_LEVELS, part, PARTS, owns, kept[at], received[at], matrices, box_gain
            )
            turn, sent = lax.optimization_barrier((turn, sent))
            received[at] = lax.ppermute(sent, "hi", [(i, i ^ 1) for i in range(4)])
        rows = rows_level(
            LOCAL_LEVELS + 1,
            part,
            PARTS,
            owns[1:],
            [kept[part, c] for c in range(images)],
            [received[part, c] for c in range(images)],
            matrices,
            box_gain,
            n_lower,
            extra,
            rows,
        )
    for partner in PARTNERS:
        pairs = [(d, d ^ partner) for d in range(4 * n_lower) if d & n_lower]
        turn = lax.ppermute(turn, ("hi", "lo"), pairs)
    own_half, rows = lax.optimization_barrier((jnp.maximum(own_half, turn), rows))
    moved = lax.all_to_all(rows.reshape(n_lower, piece + extra, images * ranks), "lo", 0, 0)
    rows = gather_rows(target_order, moved)
    rows = lax.all_to_all(rows.reshape(n_lower, piece, images * ranks), "lo", 0, 0)
    blocks = lower_levels(own_half, rows, matrices, moved, images, first_lower)
    blocks = blocks.reshape(halves, 2, images, ranks, piece)
    blocks = lax.all_to_all(blocks, "lo", 0, 0, axis_index_groups=groups)
    return to_targets(blocks, target_map.T, box_gain, 16)


def solution(mesh):
    return jax.shard_map(
        body,
        mesh=mesh,
        in_specs=(
            P(None, None, ("hi", "lo")),
            P(),
            P(),
            P(None, ("hi", "lo")),
            P(("hi", "lo"), None),
            P(),
        ),
        out_specs=P(None, None, ("hi", "lo")),
        check_vma=False,
    )
```
